32 devices in a mesh: groups: 2 (over x), radius: 16 (over z, y, core).
Axes of the slice: x: 2, y: 2, z: 4, core: 2. Of those that a mesh axis runs over, the one named last changes fastest.
Arguments:
- states: float32 [8, 400, 2048], P('groups', None, 'radius'), parts along dimension 0, may hold values from -6 to 6
- dipole: float32 [400, 400], replicated, may hold values from -0.625 to 0.625
- pattern: int32 [25, 25], replicated, may hold values 0 or 1
- angular: int32 [400], replicated, may hold values from 0 to 11
- thresholds: float32 [400], replicated, may hold values from 0 to 2
- surface_profile: float32 [2, 2048], P(None, 'radius'), may hold values from 0.2 to 1.5
- pulse_field: float32 [4], P('groups'), parts along dimension 0, may hold values from -0.05 to 0.05
Outputs:
- final_states: float32 [8, 400, 2048], P('groups', None, 'radius'), parts along dimension 0
- gradient: float32 [4], P('groups'), parts along dimension 0
The draws below stay inside these ranges and needn't reach their ends.
There are 2 independent parts, one for each index of `groups`. The reference program is written for one: setup_inputs(seed, part) draws one part's arguments, and reference() takes and returns one part's arrays. A program takes and returns all parts, laid end to end along the dimension named above; an argument that names none is the same for every part. Nothing has to cross between parts.
All inputs are finite; a program needn't handle non-finite values.
Results may differ from the reference program's by a relative error of at most 0.00019.
Values sent between devices are 32-bit elements; how exact they have to be, the bound alone decides.
A program may use at most 64 MiB of HBM per device.

```python
import math
import jax
import jax.numpy as jnp
from jax import lax

C = 400
NBLK = 25
NR = 2048
STEPS = 2
ORDER = 4


def plant(drawn, stream_key, smallest, top_value):
    extent = drawn.shape
    place = [jax.random.randint(jax.random.fold_in(stream_key, axis), (), 0, extent[axis]) for axis in range(len(extent))]
    drawn = drawn.at[tuple(place)].set(smallest)
    longest = extent.index(max(extent))
    place[longest] = (place[longest] + 1) % extent[longest]
    return drawn.at[tuple(place)].set(top_value)


def levels(key, extent, split, least, largest):
    def one(dim, parts):
        heights = jax.random.uniform(jax.random.fold_in(jax.random.fold_in(key, 6), dim), (parts,), jnp.float32, least / len(split), largest / len(split))
        return jnp.repeat(jnp.exp(heights), extent[dim] // parts).reshape((-1,) + (1,) * (len(extent) - dim - 1))

    gain = one(*split[0])
    for cut in split[1:]:
        gain = gain * one(*cut)
    return gain


def scatter_about(rng, shape, width, reach, cuts=(), kind=jnp.bfloat16):
    values = jax.random.normal(rng, shape, jnp.float32) * width
    if len(cuts) > 0:
        values = levels(rng, shape, cuts, -0.22, 0.18) * values
    return jnp.clip(values, min=-reach, max=reach).astype(kind)


def setup_inputs(seed: int = 0, part: int = 0) -> dict:
    key_list = jax.random.split(jax.random.key(seed), 8)
    own_keys = jax.random.split(jax.random.fold_in(key_list[7], part), 8)
    states = scatter_about(own_keys[0], (4, C, NR), 1.0, 6.0, ((2, 16),), jnp.float32)
    dipole = scatter_about(key_list[1], (C, C), (C // 4) ** -0.5, 0.625, (), jnp.float32)
    pattern = plant((jax.random.randint(key_list[2], (NBLK, NBLK), 0, 2) < 1).astype(jnp.int32), jax.random.fold_in(key_list[2], 1), 0, 1)
    angular = plant(jax.random.randint(key_list[3], (C,), 0, 12), jax.random.fold_in(key_list[3], 1), 0, 11).astype(jnp.int32)
    thresholds = jnp.clip(jax.random.uniform(key_list[4], (C,), jnp.float32, 0.0, 2.0), 0.0, 2.0)
    surface_profile = jnp.clip(0.2 + 1.3 * jax.random.uniform(key_list[5], (2, NR), jnp.float32) ** levels(key_list[5], (2, NR), ((1, 16),), -0.2, 0.2), 0.2, 1.5)
    pulse_field = jnp.clip(jax.random.uniform(own_keys[6], (STEPS,), jnp.float32, -0.05, 0.05), -0.05, 0.05)
    return {"states": states, "dipole": dipole, "pattern": pattern, "angular": angular, "thresholds": thresholds, "surface_profile": surface_profile, "pulse_field": pulse_field}


inner_radius = 20.0
spacing = 0.08
time_step = 0.005

def coupling_matrix(dipole, pattern, angular):
    channels = dipole.shape[0]
    blocks = pattern.shape[0]
    block_size = channels // blocks
    joined = jnp.maximum(pattern, pattern.T)
    block_owner = jnp.arange(channels, dtype=jnp.int32) // block_size
    block_pick = (block_owner[:, None] == jnp.arange(blocks, dtype=jnp.int32)[None, :]).astype(jnp.int32)
    block_mask = jnp.dot(jnp.dot(block_pick, joined), block_pick.T)
    selection = jnp.abs(angular[:, None] - angular[None, :]) == 1
    allowed = (block_mask > 0) & selection
    return jnp.where(allowed, 0.5 * (dipole + dipole.T), jnp.zeros_like(dipole))

def surface_pair(points):
    value_row = 4.0 * points[:, :, 0] - 6.0 * points[:, :, 1] + 4.0 * points[:, :, 2] - points[:, :, 3]
    slope_row = -13.0 / 3.0 * points[:, :, 0] + 9.5 * points[:, :, 1] - 7.0 * points[:, :, 2] + 11.0 / 6.0 * points[:, :, 3]
    return jnp.stack([value_row, slope_row])

def apply_hamiltonian(extended, positions, profile_rows, boundary, coupling, thresholds, centrifugal, strength, power, grid_points):
    center = extended[:, :, 2:-2]
    radial_values = inner_radius + (positions + 1).astype(jnp.float32) * spacing
    kinetic = -0.5 / (spacing * spacing) * (-1.0 / 12.0 * (extended[:, :, :-4] + extended[:, :, 4:]) + 4.0 / 3.0 * (extended[:, :, 1:-3] + extended[:, :, 3:-1]) - 2.5 * center)
    potential = (thresholds[:, None] + centrifugal[:, None] / (radial_values * radial_values)[None, :]) * center
    mixed_rows = jnp.einsum('cd,kdr->kcr', coupling, center, precision=lax.Precision.HIGHEST)
    driven = (strength * radial_values)[None, None, :] * mixed_rows
    boundary_term = boundary[0][:, :, None] * profile_rows[0][None, None, :] + boundary[1][:, :, None] * profile_rows[1][None, None, :]
    hamiltonian = kinetic + potential + driven + boundary_term
    advanced = time_step / power * jnp.stack([hamiltonian[1], -hamiltonian[0], hamiltonian[3], -hamiltonian[2]])
    inside = (positions >= 0) & (positions < grid_points)
    return (jnp.where(inside[None, None, :], advanced, jnp.zeros_like(advanced)), mixed_rows)

def reference(states, dipole, pattern, angular, thresholds, surface_profile, pulse_field):
    coupling = coupling_matrix(dipole, pattern, angular)
    centrifugal = 0.5 * (angular * (angular + 1)).astype(jnp.float32)
    positions = jnp.arange(NR, dtype=jnp.int32)
    radial_values = inner_radius + (positions + 1).astype(jnp.float32) * spacing
    normalizer = math.sqrt(C * NR) * (inner_radius + NR * spacing)
    intersections = []
    for step_index in range(STEPS):
        strength = pulse_field[step_index]
        summed = states
        taylor_term = states
        for power in range(1, ORDER + 1):
            boundary = surface_pair(taylor_term[:, :, :4])
            extended = jnp.pad(taylor_term, ((0, 0), (0, 0), (2, 2)))
            taylor_term, mixed_rows = apply_hamiltonian(extended, positions, surface_profile, boundary, coupling, thresholds, centrifugal, strength, power, NR)
            if power == 1:
                intersection = jnp.sum(radial_values[None, :] * (states[2] * mixed_rows[1] - states[3] * mixed_rows[0]))
                intersections.append(intersection)
            summed = summed + taylor_term
        states = summed
    return (states, jnp.stack(intersections) / normalizer)
```

```python
import functools
import math

import jax
import jax.numpy as jnp
from jax import lax
from jax.experimental import pallas as pl
from jax.experimental.pallas import tpu as pltpu
from jax.sharding import PartitionSpec as P

STEPS = 2
ORDER = 4
inner_radius = 20.0
spacing = 0.08
time_step = 0.005

HALO = 2 * ORDER * STEPS
STRIP = HALO + 2
BASE = 20
ROWS = 16
CHUNKS = 3
TREE = (4, 2, 1)
MESH = pl.DeviceIdType.MESH
F32 = jnp.float32
BF16 = jnp.bfloat16


def coupling_matrix(dipole, pattern, angular):
    channels = dipole.shape[0]
    blocks = pattern.shape[0]
    block_size = channels // blocks
    joined = jnp.maximum(pattern, pattern.T)
    block_mask = jnp.repeat(jnp.repeat(joined, block_size, axis=0), block_size, axis=1)
    selection = jnp.abs(angular[:, None] - angular[None, :]) == 1
    allowed = (block_mask > 0) & selection
    return jnp.where(allowed, 0.5 * (dipole + dipole.T), jnp.zeros_like(dipole))


def halves(value):
    high = value.astype(BF16)
    return high, (value - high.astype(F32)).astype(BF16)


def kernel(
    count, channels, states, lhs, chan, prof, pulse, out, grad,
    to_left, to_right, from_left, from_right, strip,
    term, total, rhs, mixed, edge, surface, pot, partial, gathered,
    halo_send, halo_recv, strip_send, strip_recv, grad_send, grad_recv,
):
    me = lax.axis_index("radius")
    size = 128
    has_left, has_right = me > 0, me < count - 1
    lane = lax.broadcasted_iota(jnp.int32, (1, size), 1)

    barrier = pltpu.get_barrier_semaphore()

    def greet(d, _):
        other = lax.rem(me + d, count)
        pl.semaphore_signal(barrier, inc=1, device_id={"radius": other}, device_id_type=MESH)
        return 0

    lax.fori_loop(1, count, greet, 0)

    low = lane < 64
    low_quarter = lax.rem(lane, 64) < 32
    padded_prof = jnp.concatenate([prof[...], jnp.zeros((6, size), F32)], axis=0)
    turned_prof = pltpu.roll(padded_prof, 64, 1)

    def pack(start, rows, parts):
        a, b, c, d = parts
        left = jnp.where(low_quarter, jnp.where(low, a, b), pltpu.roll(jnp.where(low, c, d), 32, 1))
        right = jnp.where(low_quarter, pltpu.roll(jnp.where(low, d, c), 96, 1), jnp.where(low, b, a))
        to_left[start : start + rows, :] = left
        to_right[start : start + rows, :] = right

    for start in range(0, channels, ROWS):
        rows = slice(start, start + ROWS)
        a, c = states[0, rows, :], states[2, rows, :]
        b, d = pltpu.roll(states[1, rows, :], 64, 1), pltpu.roll(states[3, rows, :], 64, 1)
        pack(start, ROWS, (a, b, c, d))
        for pair, (first, second) in enumerate(((a, b), (c, d))):
            term[pair, rows, 0:size] = first
            term[pair, rows, size : 2 * size] = second
    pack(channels, 8, (padded_prof, turned_prof, padded_prof, turned_prof))

    @pl.when(me == 0)
    def _():
        strip[...] = to_left[...]

    pl.semaphore_wait(barrier, count - 1)

    def halo_copy(source, target, which, other):
        return pltpu.make_async_remote_copy(
            src_ref=source, dst_ref=target, send_sem=halo_send.at[which],
            recv_sem=halo_recv.at[which], device_id={"radius": other}, device_id_type=MESH,
        )

    left_copy = halo_copy(to_left, from_right, 0, jnp.maximum(me - 1, 0))
    right_copy = halo_copy(to_right, from_left, 1, jnp.minimum(me + 1, count - 1))

    chunk = (channels + 8) // CHUNKS
    children = []
    for step in TREE:
        child = me + step
        mine = (lax.rem(me, 2 * step) == 0) if step < TREE[0] else (lax.rem(me, step) == 0)
        children.append((child, mine & (child < count)))

    def strip_copy(part, which):
        rows = pl.ds(part * chunk, chunk)
        return pltpu.make_async_remote_copy(
            src_ref=strip.at[rows, :], dst_ref=strip.at[rows, :],
            send_sem=strip_send.at[which, part], recv_sem=strip_recv.at[part],
            device_id={"radius": jnp.minimum(children[which][0], count - 1)}, device_id_type=MESH,
        )

    def send_on(part):
        for which in range(len(TREE)):
            @pl.when(children[which][1])
            def _():
                strip_copy(part, which).start()

    @pl.when(me == 0)
    def _():
        for part in range(CHUNKS):
            send_on(part)

    @pl.when(has_left)
    def _():
        left_copy.start()

    @pl.when(has_right)
    def _():
        right_copy.start()

    @pl.when(me > 0)
    def _():
        for part in range(CHUNKS):
            strip_copy(part, 0).wait_recv()
            send_on(part)

    second = (lane >= 48) & (lane < 112)
    place = jnp.where(second, lax.rem(lane + 64, size), lane)
    in_right, in_left = place < HALO, place >= size - HALO
    in_strip = (place >= BASE) & (place < BASE + STRIP)
    here = me * size
    extra = jnp.where(in_right, here + size + place, jnp.where(in_left, here - size + place, place - BASE))
    valid = (in_right & has_right) | (in_left & has_left) | in_strip
    extra = jnp.where(valid, extra, 0)
    keep = jnp.where(valid, 1.0, 0.0).astype(F32)
    flip = jnp.where(second, -keep, keep)
    positions = jnp.concatenate([here + lane, here + lax.rem(lane + 64, size), extra], axis=1)
    radial = inner_radius + (positions + 1).astype(F32) * spacing
    inverse = 1.0 / (radial * radial)

    @pl.when(has_right)
    def _():
        left_copy_in = halo_copy(to_left, from_right, 0, jnp.minimum(me + 1, count - 1))
        left_copy_in.wait_recv()

    @pl.when(jnp.logical_not(has_right))
    def _():
        from_right[...] = jnp.zeros_like(from_right)

    @pl.when(has_left)
    def _():
        right_copy_in = halo_copy(to_right, from_left, 1, jnp.maximum(me - 1, 0))
        right_copy_in.wait_recv()

    @pl.when(jnp.logical_not(has_left))
    def _():
        from_left[...] = jnp.zeros_like(from_left)

    def unpack(start, rows, pair):
        cut = slice(start, start + rows)
        right, left, inner = from_right[cut, :], from_left[cut, :], strip[cut, :]
        if pair == 1:
            right, left = pltpu.roll(right, 96, 1), pltpu.roll(left, 32, 1)
        inner = pltpu.roll(inner, BASE if pair == 0 else BASE + 96, 1)
        gathered_lanes = jnp.where(in_right, right, jnp.where(in_left, left, inner))
        return jnp.where(valid, gathered_lanes, 0.0)

    def shift(value, amount):
        return pltpu.roll(value, amount % size, 1)

    near = (lax.rem(lane, 64) >= BASE) & (lax.rem(lane, 64) < BASE + 4)

    def store_split(pair, start, tiles):
        for tile, value in enumerate(tiles):
            cols = slice(tile * size, (tile + 1) * size)
            high, rest = halves(value)
            rhs[pair, start : start + ROWS, cols] = high
            rhs[pair, channels + start : channels + start + ROWS, cols] = rest
            rhs[pair, 2 * channels + start : 2 * channels + start + ROWS, cols] = high
        points = jnp.where(near, tiles[2], 0.0)
        high = points.astype(BF16).astype(F32)
        rest = points - high
        edge[pair, start : start + ROWS, :] = (high + shift(rest, 8) + shift(high, 16)).astype(BF16)

    prof_extra = unpack(channels, 8, 0)
    prof_all = jnp.concatenate([padded_prof, turned_prof, prof_extra], axis=1)
    row = lax.broadcasted_iota(jnp.int32, (size, 1), 0)
    offset = lax.rem(row, 64) - BASE
    point = lax.rem(offset + 64, 8)
    used = (offset >= 0) & (offset < 24) & (point < 4)

    def weights(values):
        found = jnp.zeros((size, 1), F32)
        for index, value in enumerate(values):
            found = jnp.where(used & (point == index), value, found)
        return found

    value_weight = weights((4.0, -6.0, 4.0, -1.0))
    slope_weight = weights((-13.0 / 3.0, 9.5, -7.0, 11.0 / 6.0))
    owner = jnp.concatenate([jnp.zeros((1, size), jnp.int32), jnp.ones((1, size), jnp.int32), second.astype(jnp.int32)], axis=1)
    full = value_weight * prof_all[0:1, :] + slope_weight * prof_all[1:2, :]
    full = jnp.where((row // 64) == owner, full, 0.0)
    high = full.astype(BF16).astype(F32)
    surface[...] = jnp.where(offset < 16, high, full - high).astype(BF16)

    rhs[:, 3 * channels :, :] = jnp.zeros((2, rhs.shape[1] - 3 * channels, 3 * size), BF16)
    diagonal = 1.25 / (spacing * spacing)
    for start in range(0, channels, ROWS):
        rows = slice(start, start + ROWS)
        pot[rows, :] = chan[rows, 0:1] + chan[rows, 1:2] * inverse + diagonal
        for pair in range(2):
            tiles = [term[pair, rows, 0:size], term[pair, rows, size : 2 * size], unpack(start, ROWS, pair)]
            term[pair, rows, 2 * size :] = tiles[2]
            store_split(pair, start, tiles)
            total[0, pair, rows, :] = jnp.concatenate(tiles, axis=1)
            total[1, pair, rows, :] = jnp.zeros((ROWS, 3 * size), F32)

    far_weight = 0.5 / (spacing * spacing) / 12.0
    near_weight = -0.5 / (spacing * spacing) * 4.0 / 3.0

    def stencil(first, other, extra_tile):
        results = [None] * 3
        for distance, weight in ((1, near_weight), (2, far_weight)):
            for amount in (distance, -distance):
                ra, rb, rx = shift(first, amount), shift(other, amount), shift(extra_tile, amount)
                if amount > 0:
                    seam = lane < amount
                    middle = (lane >= 64) & (lane < 64 + amount)
                else:
                    seam = lane >= size + amount
                    middle = (lane >= 64 + amount) & (lane < 64)
                moved = (
                    jnp.where(seam, rx, ra),
                    jnp.where(middle, rx, rb),
                    jnp.where(seam, ra, jnp.where(middle, rb, rx)),
                )
                if amount > 0:
                    ahead = moved
            for tile in range(3):
                both = weight * (ahead[tile] + moved[tile])
                results[tile] = both if results[tile] is None else results[tile] + both
        return results

    def grad_copy(other, slot):
        return pltpu.make_async_remote_copy(
            src_ref=partial, dst_ref=gathered.at[slot], send_sem=grad_send.at[other],
            recv_sem=grad_recv.at[slot], device_id={"radius": other}, device_id_type=MESH,
        )

    def one_step(step, _):
        strength = pulse[step]
        driven = strength * radial

        def one_term(index, _):
            power = index + 1
            scale = time_step / power.astype(F32)
            odd = lax.rem(power, 2)
            signed = jnp.where(odd == 1, -scale, scale)
            for pair in range(2):
                mixed[pair] = jnp.dot(lhs[...], rhs[pair], preferred_element_type=F32)

            @pl.when(index == 0)
            def _():
                found = jnp.zeros((8, size), F32)
                for start in range(0, channels, ROWS):
                    rows = slice(start, start + ROWS)
                    turned = shift(mixed[0, rows, size : 2 * size], 64) * term[1, rows, 0:size]
                    straight = shift(term[1, rows, size : 2 * size], 64) * mixed[0, rows, 0:size]
                    both = turned - straight
                    found = found + both[0:8] + both[8:16]
                partial[step] = found * radial[:, 0:size]

                @pl.when(step == STEPS - 1)
                def _():
                    def send(d, _):
                        grad_copy(lax.rem(me + d, count), me).start()
                        return 0

                    lax.fori_loop(1, count, send, 0)

            for pair in range(2):
                bound = jnp.dot(edge[pair], surface[...], preferred_element_type=F32)
                for start in range(0, channels, ROWS):
                    rows = slice(start, start + ROWS)
                    now = [term[pair, rows, t * size : (t + 1) * size] for t in range(3)]
                    moved = stencil(*now)
                    new = []
                    for tile in range(3):
                        cols = slice(tile * size, (tile + 1) * size)
                        value = moved[tile] + pot[rows, cols] * now[tile]
                        value = value + driven[:, cols] * mixed[pair, rows, cols] + bound[rows, cols]
                        factor = (signed, -signed, signed * flip)[tile]
                        value = factor * value
                        new.append(value)
                        term[pair, rows, cols] = value
                        total[odd, pair, rows, cols] += value
                    store_split(pair, start, new)
            return 0

        lax.fori_loop(0, ORDER, one_term, 0)

        for pair in range(2):
            for start in range(0, channels, ROWS):
                rows = slice(start, start + ROWS)
                tiles = []
                for tile in range(3):
                    cols = slice(tile * size, (tile + 1) * size)
                    source = (1, 0, 2)[tile]
                    turned = shift(total[1, pair, rows, source * size : (source + 1) * size], 64)
                    tiles.append(total[0, pair, rows, cols] + turned)
                for tile in range(3):
                    cols = slice(tile * size, (tile + 1) * size)
                    term[pair, rows, cols] = tiles[tile]
                    total[0, pair, rows, cols] = tiles[tile]
                    total[1, pair, rows, cols] = jnp.zeros((ROWS, size), F32)
                store_split(pair, start, tiles)
        return 0

    lax.fori_loop(0, STEPS, one_step, 0)

    for pair in range(2):
        for start in range(0, channels, ROWS):
            rows = slice(start, start + ROWS)
            out[2 * pair, rows, :] = term[pair, rows, 0:size]
            out[2 * pair + 1, rows, :] = shift(term[pair, rows, size : 2 * size], 64)

    gathered[me] = partial[...]

    def collect(d, _):
        other = lax.rem(me + d, count)
        copy = grad_copy(other, other)
        copy.wait_recv()
        return 0

    lax.fori_loop(1, count, collect, 0)
    normalizer = math.sqrt(channels * count * size) * (inner_radius + count * size * spacing)
    for step in range(STEPS):
        found = jnp.zeros((8, size), F32)
        for index in range(count):
            found = found + gathered[index, step]
        grad[step] = jnp.sum(found) / normalizer

    def finish(d, _):
        grad_copy(lax.rem(me + d, count), me).wait_send()
        return 0

    lax.fori_loop(1, count, finish, 0)

    @pl.when(has_left)
    def _():
        left_copy.wait_send()

    @pl.when(has_right)
    def _():
        right_copy.wait_send()

    for which in range(len(TREE)):
        @pl.when(children[which][1])
        def _():
            for part in range(CHUNKS):
                strip_copy(part, which).wait_send()


def per_device(count, states, dipole, pattern, angular, thresholds, surface_profile, pulse_field):
    channels = states.shape[1]
    size = states.shape[2]
    coupling = coupling_matrix(dipole, pattern, angular)
    rounded = lax.reduce_precision(coupling, 8, 7)
    high, rest = rounded.astype(BF16), (coupling - rounded).astype(BF16)
    depth = -(-3 * channels // 256) * 256
    lhs = jnp.concatenate([high, high, rest, jnp.zeros((channels, depth - 3 * channels), BF16)], axis=1)
    centrifugal = 0.5 * (angular * (angular + 1)).astype(F32)
    chan = jnp.stack([thresholds, centrifugal], axis=1)
    vmem = pl.BlockSpec(memory_space=pltpu.VMEM)
    smem = pl.BlockSpec(memory_space=pltpu.SMEM)
    message = pltpu.VMEM((channels + 8, size), F32)
    wide = (2, channels, 3 * size)
    return pl.pallas_call(
        functools.partial(kernel, count, channels),
        out_shape=(
            jax.ShapeDtypeStruct(states.shape, F32),
            jax.ShapeDtypeStruct(pulse_field.shape, F32),
        ),
        in_specs=[vmem, vmem, vmem, vmem, smem],
        out_specs=(vmem, smem),
        scratch_shapes=[
            message, message, message, message, message,
            pltpu.VMEM(wide, F32),
            pltpu.VMEM((2,) + wide, F32),
            pltpu.VMEM((2, depth, 3 * size), BF16),
            pltpu.VMEM(wide, F32),
            pltpu.VMEM((2, channels, size), BF16),
            pltpu.VMEM((size, 3 * size), BF16),
            pltpu.VMEM((channels, 3 * size), F32),
            pltpu.VMEM((STEPS, 8, size), F32),
            pltpu.VMEM((count, STEPS, 8, size), F32),
            pltpu.SemaphoreType.DMA((2,)),
            pltpu.SemaphoreType.DMA((2,)),
            pltpu.SemaphoreType.DMA((len(TREE), CHUNKS)),
            pltpu.SemaphoreType.DMA((CHUNKS,)),
            pltpu.SemaphoreType.DMA((count,)),
            pltpu.SemaphoreType.DMA((count,)),
        ],
        compiler_params=pltpu.CompilerParams(
            collective_id=0, has_side_effects=True, vmem_limit_bytes=48 * 1024 * 1024
        ),
        cost_estimate=pl.CostEstimate(flops=8000000000, bytes_accessed=4000000, transcendentals=0),
    )(states, lhs, chan, surface_profile, pulse_field)


def solution(mesh):
    return jax.shard_map(
        functools.partial(per_device, mesh.shape["radius"]),
        mesh=mesh,
        in_specs=(P("groups", None, "radius"), P(), P(), P(), P(), P(None, "radius"), P("groups")),
        out_specs=(P("groups", None, "radius"), P("groups")),
        check_vma=False,
    )
```

```python
import functools
import math

import jax
import jax.numpy as jnp
from jax import lax
from jax.experimental import pallas as pl
from jax.experimental.pallas import tpu as pltpu
from jax.sharding import PartitionSpec as P

STEPS = 2
ORDER = 4
inner_radius = 20.0
spacing = 0.08
time_step = 0.005

HALO = 2 * ORDER * STEPS
STRIP = HALO + 2
BASE = 20
ROWS = 16
CHUNKS = 13
BLOCK = 128
TREE = (4, 2, 1)
MESH = pl.DeviceIdType.MESH
F32 = jnp.float32
BF16 = jnp.bfloat16


def halves(value):
    high = value.astype(BF16)
    return high, (value - high.astype(F32)).astype(BF16)


def build_coupling(channels, dipole, pattern, angular, thresholds, square, joined, columns, lhs):
    blocks = pattern.shape[0]
    parts = square.shape[0] // BLOCK
    owned = channels // blocks
    square[...] = jnp.zeros_like(square)
    square[0:channels, 0:channels] = dipole[...]
    joined[...] = jnp.zeros_like(joined)
    joined[0:blocks, 0:blocks] = pattern[...].astype(F32)
    either = jnp.maximum(joined[...], joined[...].T).astype(BF16)
    lane = lax.broadcasted_iota(jnp.int32, (BLOCK, BLOCK), 1)
    row = lax.broadcasted_iota(jnp.int32, (BLOCK, BLOCK), 0)

    def pick(part):
        return jnp.where((row + part * BLOCK) // owned == lane, 1.0, 0.0).astype(BF16)

    def spread(ref, part):
        return jnp.broadcast_to(ref[part : part + 1, :], (BLOCK, BLOCK))

    across = [spread(angular, part) for part in range(parts)]
    picks = [pick(part) for part in range(parts)]
    for i in range(parts):
        down = across[i].T
        rows = slice(i * BLOCK, (i + 1) * BLOCK)
        columns[0, rows, :] = spread(thresholds, i).T
        columns[1, rows, :] = 0.5 * (down * (down + 1.0))
        held = jnp.dot(picks[i], either, preferred_element_type=F32).astype(BF16)
        for j in range(parts):
            cols = slice(j * BLOCK, (j + 1) * BLOCK)
            mask = lax.dot_general(held, picks[j], (((1,), (1,)), ((), ())), preferred_element_type=F32)
            allowed = (mask > 0.5) & (jnp.abs(down - across[j]) == 1.0)
            mean = 0.5 * (square[rows, cols] + square[cols, rows].T)
            coupling = jnp.where(allowed, mean, 0.0)
            high = coupling.astype(BF16).astype(F32)
            rest = coupling - high
            if j < parts - 1:
                for copy, value in enumerate((high, high, rest)):
                    place = copy * (parts - 1) * BLOCK + j * BLOCK
                    lhs[rows, place : place + BLOCK] = value.astype(BF16)
            else:
                left = channels - j * BLOCK
                mixed = jnp.where(lane < left, high, 0.0)
                mixed = jnp.where((lane >= left) & (lane < 2 * left), pltpu.roll(high, left, 1), mixed)
                mixed = jnp.where((lane >= 2 * left) & (lane < 3 * left), pltpu.roll(rest, 2 * left, 1), mixed)
                lhs[rows, 3 * j * BLOCK :] = mixed.astype(BF16)


def kernel(
    count, channels, states, dipole, pattern, angular, thresholds, prof, pulse, out, grad,
    to_left, to_right, from_left, from_right, strip,
    term, total, rhs, mixed, bound, edge, surface, pot, partial, gathered,
    lhs, square, joined, columns,
    halo_send, halo_recv, strip_send, strip_recv, grad_send, grad_recv,
):
    me = lax.axis_index("radius")
    size = 128
    has_left, has_right = me > 0, me < count - 1
    lane = lax.broadcasted_iota(jnp.int32, (ROWS, size), 1)
    row_lane = lane[0:1, :]
    tail = channels // BLOCK * BLOCK
    extra_rows = 16

    def over_rows(body, carry=0):
        return lax.fori_loop(0, channels // ROWS, lambda i, c: body(pl.multiple_of(i * ROWS, ROWS), c), carry)

    barrier = pltpu.get_barrier_semaphore()

    def greet(d, _):
        other = lax.rem(me + d, count)
        pl.semaphore_signal(barrier, inc=1, device_id={"radius": other}, device_id_type=MESH)
        return 0

    lax.fori_loop(1, count, greet, 0)

    low = lane < 64
    low_quarter = lax.rem(lane, 64) < 32
    padded_prof = jnp.concatenate([prof[...], jnp.zeros((extra_rows - 2, size), F32)], axis=0)
    turned_prof = pltpu.roll(padded_prof, 64, 1)

    def pack(rows, parts):
        a, b, c, d = parts
        left = jnp.where(low_quarter, jnp.where(low, a, b), pltpu.roll(jnp.where(low, c, d), 32, 1))
        right = jnp.where(low_quarter, pltpu.roll(jnp.where(low, d, c), 96, 1), jnp.where(low, b, a))
        to_left[rows, :] = left
        to_right[rows, :] = right

    def pack_rows(start, carry):
        rows = pl.ds(start, ROWS)
        a, c = states[0, rows, :], states[2, rows, :]
        b, d = pltpu.roll(states[1, rows, :], 64, 1), pltpu.roll(states[3, rows, :], 64, 1)
        pack(rows, (a, b, c, d))
        for pair, (first, other) in enumerate(((a, b), (c, d))):
            term[pair, rows, 0:size] = first
            term[pair, rows, size : 2 * size] = other
        return carry

    over_rows(pack_rows)
    pack(slice(channels, channels + extra_rows), (padded_prof, turned_prof, padded_prof, turned_prof))

    @pl.when(me == 0)
    def _():
        strip[...] = to_left[...]

    pl.semaphore_wait(barrier, count - 1)

    def halo_copy(source, target, which, other):
        return pltpu.make_async_remote_copy(
            src_ref=source, dst_ref=target, send_sem=halo_send.at[which],
            recv_sem=halo_recv.at[which], device_id={"radius": other}, device_id_type=MESH,
        )

    left_copy = halo_copy(to_left, from_right, 0, jnp.maximum(me - 1, 0))
    right_copy = halo_copy(to_right, from_left, 1, jnp.minimum(me + 1, count - 1))

    chunk = (channels + extra_rows) // CHUNKS
    children = []
    for step in TREE:
        child = me + step
        mine = (lax.rem(me, 2 * step) == 0) if step < TREE[0] else (lax.rem(me, step) == 0)
        children.append((child, mine & (child < count)))

    def strip_copy(part, which):
        rows = pl.ds(part * chunk, chunk)
        return pltpu.make_async_remote_copy(
            src_ref=strip.at[rows, :], dst_ref=strip.at[rows, :],
            send_sem=strip_send.at[which, part], recv_sem=strip_recv.at[part],
            device_id={"radius": jnp.minimum(children[which][0], count - 1)}, device_id_type=MESH,
        )

    def send_on(part):
        for which in range(len(TREE)):
            @pl.when(children[which][1])
            def _():
                strip_copy(part, which).start()

    @pl.when(me == 0)
    def _():
        for part in range(CHUNKS):
            send_on(part)

    @pl.when(has_left)
    def _():
        left_copy.start()

    @pl.when(has_right)
    def _():
        right_copy.start()

    build_coupling(channels, dipole, pattern, angular, thresholds, square, joined, columns, lhs)

    @pl.when(me > 0)
    def _():
        for part in range(CHUNKS):
            strip_copy(part, 0).wait_recv()
            send_on(part)

    second = (lane >= 48) & (lane < 112)
    place = jnp.where(second, lax.rem(lane + 64, size), lane)
    in_right, in_left = place < HALO, place >= size - HALO
    in_strip = (place >= BASE) & (place < BASE + STRIP)
    here = me * size
    extra = jnp.where(in_right, here + size + place, jnp.where(in_left, here - size + place, place - BASE))
    valid = (in_right & has_right) | (in_left & has_left) | in_strip
    extra = jnp.where(valid, extra, 0)
    keep = jnp.where(valid, 1.0, 0.0).astype(F32)
    flip = jnp.where(second, -keep, keep)
    positions = jnp.concatenate([here + row_lane, here + lax.rem(row_lane + 64, size), extra[0:1, :]], axis=1)
    radial = inner_radius + (positions + 1).astype(F32) * spacing
    inverse = 1.0 / (radial * radial)

    @pl.when(has_right)
    def _():
        left_copy_in = halo_copy(to_left, from_right, 0, jnp.minimum(me + 1, count - 1))
        left_copy_in.wait_recv()

    @pl.when(jnp.logical_not(has_right))
    def _():
        from_right[...] = jnp.zeros_like(from_right)

    @pl.when(has_left)
    def _():
        right_copy_in = halo_copy(to_right, from_left, 1, jnp.maximum(me - 1, 0))
        right_copy_in.wait_recv()

    @pl.when(jnp.logical_not(has_left))
    def _():
        from_left[...] = jnp.zeros_like(from_left)

    def unpack(cut, pair):
        right, left, inner = from_right[cut, :], from_left[cut, :], strip[cut, :]
        if pair == 1:
            right, left = pltpu.roll(right, 96, 1), pltpu.roll(left, 32, 1)
        inner = pltpu.roll(inner, BASE if pair == 0 else BASE + 96, 1)
        found = jnp.where(in_right, right, jnp.where(in_left, left, inner))
        return jnp.where(valid, found, 0.0)

    def shift(value, amount):
        return pltpu.roll(value, amount % size, 1)

    near = (lax.rem(lane, 64) >= BASE) & (lax.rem(lane, 64) < BASE + 4)

    def store_split(pair, start, tiles):
        whole = start < tail
        first = pl.multiple_of(jnp.where(whole, start, 3 * tail), ROWS)
        stride = jnp.where(whole, tail, ROWS)
        for tile, value in enumerate(tiles):
            cols = slice((3 * pair + tile) * size, (3 * pair + tile + 1) * size)
            high, rest = halves(value)
            rhs[pl.ds(first, ROWS), cols] = high
            rhs[pl.ds(pl.multiple_of(first + stride, ROWS), ROWS), cols] = rest
            rhs[pl.ds(pl.multiple_of(first + 2 * stride, ROWS), ROWS), cols] = high
        points = jnp.where(near, tiles[2], 0.0)
        high = points.astype(BF16).astype(F32)
        rest = points - high
        edge[pair, pl.ds(start, ROWS), :] = (high + shift(rest, 8) + shift(high, 16)).astype(BF16)

    prof_extra = unpack(slice(channels, channels + extra_rows), 0)
    prof_all = jnp.concatenate([padded_prof, turned_prof, prof_extra], axis=1)
    row = lax.broadcasted_iota(jnp.int32, (size, 1), 0)
    offset = lax.rem(row, 64) - BASE
    point = lax.rem(offset + 64, 8)
    used = (offset >= 0) & (offset < 24) & (point < 4)

    def weights(values):
        found = jnp.zeros((size, 1), F32)
        for index, value in enumerate(values):
            found = jnp.where(used & (point == index), value, found)
        return found

    value_weight = weights((4.0, -6.0, 4.0, -1.0))
    slope_weight = weights((-13.0 / 3.0, 9.5, -7.0, 11.0 / 6.0))
    owner = jnp.concatenate([jnp.zeros((1, size), jnp.int32), jnp.ones((1, size), jnp.int32), jnp.where(second, 1, 0)[0:1, :]], axis=1)
    full = value_weight * prof_all[0:1, :] + slope_weight * prof_all[1:2, :]
    full = jnp.where((row // 64) == owner, full, 0.0)
    high = full.astype(BF16).astype(F32)
    surface[...] = jnp.where(offset < 16, high, full - high).astype(BF16)

    rhs[3 * channels :, :] = jnp.zeros((rhs.shape[0] - 3 * channels, 6 * size), BF16)
    diagonal = 1.25 / (spacing * spacing)

    def begin(start, carry):
        rows = pl.ds(start, ROWS)
        for tile in range(3):
            cols = slice(tile * size, (tile + 1) * size)
            pot[rows, cols] = columns[0, rows, :] + columns[1, rows, :] * inverse[:, cols] + diagonal
        for pair in range(2):
            tiles = [term[pair, rows, 0:size], term[pair, rows, size : 2 * size], unpack(rows, pair)]
            term[pair, rows, 2 * size :] = tiles[2]
            store_split(pair, start, tiles)
            total[0, pair, rows, :] = jnp.concatenate(tiles, axis=1)
            total[1, pair, rows, :] = jnp.zeros((ROWS, 3 * size), F32)
        return carry

    over_rows(begin)

    far_weight = 0.5 / (spacing * spacing) / 12.0
    near_weight = -0.5 / (spacing * spacing) * 4.0 / 3.0

    def stencil(first, other, extra_tile):
        results = [None] * 3
        for distance, weight in ((1, near_weight), (2, far_weight)):
            for amount in (distance, -distance):
                ra, rb, rx = shift(first, amount), shift(other, amount), shift(extra_tile, amount)
                if amount > 0:
                    seam = lane < amount
                    middle = (lane >= 64) & (lane < 64 + amount)
                else:
                    seam = lane >= size + amount
                    middle = (lane >= 64 + amount) & (lane < 64)
                moved = (
                    jnp.where(seam, rx, ra),
                    jnp.where(middle, rx, rb),
                    jnp.where(seam, ra, jnp.where(middle, rb, rx)),
                )
                if amount > 0:
                    ahead = moved
            for tile in range(3):
                both = weight * (ahead[tile] + moved[tile])
                results[tile] = both if results[tile] is None else results[tile] + both
        return results

    def grad_copy(other, slot):
        return pltpu.make_async_remote_copy(
            src_ref=partial, dst_ref=gathered.at[slot], send_sem=grad_send.at[other],
            recv_sem=grad_recv.at[slot], device_id={"radius": other}, device_id_type=MESH,
        )

    def one_step(step, _):
        strength = pulse[step]
        driven = strength * radial

        def one_term(index, _):
            power = index + 1
            scale = time_step / power.astype(F32)
            odd = lax.rem(power, 2)
            signed = jnp.where(odd == 1, -scale, scale)

            def mix(block, carry):
                cols = pl.ds(pl.multiple_of(block * 256, 256), 256)
                mixed[:, cols] = jnp.dot(lhs[0:channels, :], rhs[:, cols], preferred_element_type=F32)
                return carry

            lax.fori_loop(0, 3, mix, 0)

            def border(pair, carry):
                bound[pair] = jnp.dot(edge[pair], surface[...], preferred_element_type=F32)
                return carry

            lax.fori_loop(0, 2, border, 0)

            @pl.when(index == 0)
            def _():
                def meet(start, found):
                    rows = pl.ds(start, ROWS)
                    turned = shift(mixed[rows, size : 2 * size], 64) * term[1, rows, 0:size]
                    straight = shift(term[1, rows, size : 2 * size], 64) * mixed[rows, 0:size]
                    both = turned - straight
                    return found + both[0:8] + both[8:16]

                partial[step] = over_rows(meet, jnp.zeros((8, size), F32)) * radial[:, 0:size]

                @pl.when(step == STEPS - 1)
                def _():
                    def send(d, _):
                        grad_copy(lax.rem(me + d, count), me).start()
                        return 0

                    lax.fori_loop(1, count, send, 0)

            def advance(start, carry):
                rows = pl.ds(start, ROWS)
                for pair in range(2):
                    now = [term[pair, rows, t * size : (t + 1) * size] for t in range(3)]
                    moved = stencil(*now)
                    new = []
                    for tile in range(3):
                        cols = slice(tile * size, (tile + 1) * size)
                        wide = slice((3 * pair + tile) * size, (3 * pair + tile + 1) * size)
                        value = moved[tile] + pot[rows, cols] * now[tile]
                        value = value + driven[:, cols] * mixed[rows, wide] + bound[pair, rows, cols]
                        factor = (signed, -signed, signed * flip)[tile]
                        value = factor * value
                        new.append(value)
                        term[pair, rows, cols] = value
                        total[odd, pair, rows, cols] += value
                    store_split(pair, start, new)
                return carry

            over_rows(advance)
            return 0

        lax.fori_loop(0, ORDER, one_term, 0)

        def close(start, carry):
            rows = pl.ds(start, ROWS)
            for pair in range(2):
                tiles = []
                for tile in range(3):
                    cols = slice(tile * size, (tile + 1) * size)
                    source = (1, 0, 2)[tile]
                    turned = shift(total[1, pair, rows, source * size : (source + 1) * size], 64)
                    tiles.append(total[0, pair, rows, cols] + turned)
                for tile in range(3):
                    cols = slice(tile * size, (tile + 1) * size)
                    term[pair, rows, cols] = tiles[tile]
                    total[0, pair, rows, cols] = tiles[tile]
                    total[1, pair, rows, cols] = jnp.zeros((ROWS, size), F32)
                store_split(pair, start, tiles)
            return carry

        over_rows(close)
        return 0

    lax.fori_loop(0, STEPS, one_step, 0)

    def finish_rows(start, carry):
        rows = pl.ds(start, ROWS)
        for pair in range(2):
            out[2 * pair, rows, :] = term[pair, rows, 0:size]
            out[2 * pair + 1, rows, :] = shift(term[pair, rows, size : 2 * size], 64)
        return carry

    over_rows(finish_rows)

    gathered[me] = partial[...]

    def collect(d, _):
        other = lax.rem(me + d, count)
        copy = grad_copy(other, other)
        copy.wait_recv()
        return 0

    lax.fori_loop(1, count, collect, 0)
    normalizer = math.sqrt(channels * count * size) * (inner_radius + count * size * spacing)
    for step in range(STEPS):
        found = jnp.zeros((8, size), F32)
        for index in range(count):
            found = found + gathered[index, step]
        grad[step] = jnp.sum(found) / normalizer

    def finish(d, _):
        grad_copy(lax.rem(me + d, count), me).wait_send()
        return 0

    lax.fori_loop(1, count, finish, 0)

    @pl.when(has_left)
    def _():
        left_copy.wait_send()

    @pl.when(has_right)
    def _():
        right_copy.wait_send()

    for which in range(len(TREE)):
        @pl.when(children[which][1])
        def _():
            for part in range(CHUNKS):
                strip_copy(part, which).wait_send()


def per_device(count, states, dipole, pattern, angular, thresholds, surface_profile, pulse_field):
    channels = states.shape[1]
    size = states.shape[2]
    padded = -(-channels // BLOCK) * BLOCK
    depth = 3 * (padded - BLOCK) + BLOCK
    fill = (0, padded - channels)
    angular = jnp.pad(angular.astype(F32), fill).reshape(-1, BLOCK)
    thresholds = jnp.pad(thresholds, fill).reshape(-1, BLOCK)
    vmem = pl.BlockSpec(memory_space=pltpu.VMEM)
    smem = pl.BlockSpec(memory_space=pltpu.SMEM)
    message = pltpu.VMEM((channels + 16, size), F32)
    wide = (2, channels, 3 * size)
    return pl.pallas_call(
        functools.partial(kernel, count, channels),
        out_shape=(
            jax.ShapeDtypeStruct(states.shape, F32),
            jax.ShapeDtypeStruct(pulse_field.shape, F32),
        ),
        in_specs=[vmem] * 6 + [smem],
        out_specs=(vmem, smem),
        scratch_shapes=[
            message, message, message, message, message,
            pltpu.VMEM(wide, F32),
            pltpu.VMEM((2,) + wide, F32),
            pltpu.VMEM((depth, 6 * size), BF16),
            pltpu.VMEM((channels, 6 * size), F32),
            pltpu.VMEM(wide, F32),
            pltpu.VMEM((2, channels, size), BF16),
            pltpu.VMEM((size, 3 * size), BF16),
            pltpu.VMEM((channels, 3 * size), F32),
            pltpu.VMEM((STEPS, 8, size), F32),
            pltpu.VMEM((count, STEPS, 8, size), F32),
            pltpu.VMEM((padded, depth), BF16),
            pltpu.VMEM((padded, padded), F32),
            pltpu.VMEM((BLOCK, BLOCK), F32),
            pltpu.VMEM((2, padded, BLOCK), F32),
            pltpu.SemaphoreType.DMA((2,)),
            pltpu.SemaphoreType.DMA((2,)),
            pltpu.SemaphoreType.DMA((len(TREE), CHUNKS)),
            pltpu.SemaphoreType.DMA((CHUNKS,)),
            pltpu.SemaphoreType.DMA((count,)),
            pltpu.SemaphoreType.DMA((count,)),
        ],
        compiler_params=pltpu.CompilerParams(
            collective_id=0, has_side_effects=True, vmem_limit_bytes=48 * 1024 * 1024
        ),
        cost_estimate=pl.CostEstimate(flops=8000000000, bytes_accessed=4000000, transcendentals=0),
    )(states, dipole, pattern, angular, thresholds, surface_profile, pulse_field)


def solution(mesh):
    return jax.shard_map(
        functools.partial(per_device, mesh.shape["radius"]),
        mesh=mesh,
        in_specs=(P("groups", None, "radius"), P(), P(), P(), P(), P(None, "radius"), P("groups")),
        out_specs=(P("groups", None, "radius"), P("groups")),
        check_vma=False,
    )
```

```python
import functools
import math

import jax
import jax.numpy as jnp
from jax import lax
from jax.experimental import pallas as pl
from jax.experimental.pallas import tpu as pltpu
from jax.sharding import PartitionSpec as P

STEPS = 2
ORDER = 4
inner_radius = 20.0
spacing = 0.08
time_step = 0.005

HALO = 2 * ORDER * STEPS
STRIP = HALO + 2
BASE = 20
ROWS = 16
CHUNKS = 13
BLOCK = 128
GROUP = 5
TREE = (4, 2, 1)
MESH = pl.DeviceIdType.MESH
F32 = jnp.float32
BF16 = jnp.bfloat16


def halves(value):
    high = value.astype(BF16)
    return high, (value - high.astype(F32)).astype(BF16)


def build_coupling(channels, dipole, pattern, chan, square, joined, columns, lhs):
    blocks = pattern.shape[0]
    parts = square.shape[0] // BLOCK
    owned = channels // blocks
    square[...] = jnp.zeros_like(square)
    square[0:channels, 0:channels] = dipole[...]
    joined[...] = jnp.zeros_like(joined)
    joined[0:blocks, 0:blocks] = pattern[...].astype(F32)
    either = jnp.maximum(joined[...], joined[...].T).astype(BF16)
    lane = lax.broadcasted_iota(jnp.int32, (BLOCK, BLOCK), 1)
    row = lax.broadcasted_iota(jnp.int32, (BLOCK, BLOCK), 0)

    def pick(part):
        return jnp.where((row + part * BLOCK) // owned == lane, 1.0, 0.0).astype(BF16)

    def spread(ref, part):
        return jnp.broadcast_to(ref[part : part + 1, :], (BLOCK, BLOCK))

    across = [spread(chan, part) for part in range(parts)]
    picks = [pick(part) for part in range(parts)]
    for i in range(parts):
        down = across[i].T
        rows = slice(i * BLOCK, (i + 1) * BLOCK)
        columns[0, rows, :] = spread(chan, parts + i).T
        columns[1, rows, :] = 0.5 * (down * (down + 1.0))
        held = jnp.dot(picks[i], either, preferred_element_type=F32).astype(BF16)
        found = {}
        for j in range(parts):
            cols = slice(j * BLOCK, (j + 1) * BLOCK)
            mask = lax.dot_general(held, picks[j], (((1,), (1,)), ((), ())), preferred_element_type=F32)
            allowed = (mask > 0.5) & (jnp.abs(down - across[j]) == 1.0)
            mean = 0.5 * (square[rows, cols] + square[cols, rows].T)
            coupling = jnp.where(allowed, mean, 0.0)
            high = coupling.astype(BF16).astype(F32)
            rest = coupling - high
            for copy, value in enumerate((high, high, rest)):
                place = copy * channels + j * BLOCK
                tile, off = place // BLOCK, place % BLOCK
                moved = pltpu.roll(value, off, 1) if off else value
                for tile, kept in ((tile, lane >= off), (tile + 1, lane < off)):
                    if tile in found:
                        found[tile] = found[tile] + jnp.where(kept, moved, 0.0)
                    elif tile < lhs.shape[1] // BLOCK:
                        found[tile] = jnp.where(kept, moved, 0.0)
        for tile, value in found.items():
            lhs[rows, tile * BLOCK : (tile + 1) * BLOCK] = value.astype(BF16)


def kernel(
    count, channels, states_in, dipole_in, pattern_in, chan_in, prof_in, pulse, out, grad,
    to_left, to_right, from_left, from_right, strip,
    term, total, rhs, mixed, bound, surface, pot, partial, gathered,
    lhs, square, joined, columns, states, dipole, pattern, chan, prof, load,
    halo_send, halo_recv, strip_send, strip_recv, grad_send, grad_recv,
):
    me = lax.axis_index("radius")
    size = 128
    has_left, has_right = me > 0, me < count - 1
    lane = lax.broadcasted_iota(jnp.int32, (ROWS, size), 1)
    row_lane = lane[0:1, :]
    extra_rows = 16
    loads = [
        pltpu.make_async_copy(source, target, load.at[which])
        for which, (source, target) in enumerate(
            ((states_in, states), (prof_in, prof), (dipole_in, dipole), (pattern_in, pattern), (chan_in, chan))
        )
    ]
    for copy in loads:
        copy.start()

    def over_rows(body, carry=0):
        def several(index, carry):
            for part in range(GROUP):
                carry = body(pl.multiple_of((index * GROUP + part) * ROWS, ROWS), carry)
            return carry

        return lax.fori_loop(0, channels // ROWS // GROUP, several, carry)

    barrier = pltpu.get_barrier_semaphore()

    def greet(d, _):
        other = lax.rem(me + d, count)
        pl.semaphore_signal(barrier, inc=1, device_id={"radius": other}, device_id_type=MESH)
        return 0

    lax.fori_loop(1, count, greet, 0)

    loads[0].wait()
    loads[1].wait()
    low = lane < 64
    low_quarter = lax.rem(lane, 64) < 32
    padded_prof = jnp.concatenate([prof[...], jnp.zeros((extra_rows - 2, size), F32)], axis=0)
    turned_prof = pltpu.roll(padded_prof, 64, 1)

    def pack(rows, parts):
        a, b, c, d = parts
        left = jnp.where(low_quarter, jnp.where(low, a, b), pltpu.roll(jnp.where(low, c, d), 32, 1))
        right = jnp.where(low_quarter, pltpu.roll(jnp.where(low, d, c), 96, 1), jnp.where(low, b, a))
        to_left[rows, :] = left
        to_right[rows, :] = right

    def pack_rows(start, carry):
        rows = pl.ds(start, ROWS)
        a, c = states[0, rows, :], states[2, rows, :]
        b, d = pltpu.roll(states[1, rows, :], 64, 1), pltpu.roll(states[3, rows, :], 64, 1)
        pack(rows, (a, b, c, d))
        for pair, (first, other) in enumerate(((a, b), (c, d))):
            term[pair, rows, 0:size] = first
            term[pair, rows, size : 2 * size] = other
        return carry

    over_rows(pack_rows)
    pack(slice(channels, channels + extra_rows), (padded_prof, turned_prof, padded_prof, turned_prof))

    @pl.when(me == 0)
    def _():
        strip[...] = to_left[...]

    pl.semaphore_wait(barrier, count - 1)

    def halo_copy(source, target, which, other):
        return pltpu.make_async_remote_copy(
            src_ref=source, dst_ref=target, send_sem=halo_send.at[which],
            recv_sem=halo_recv.at[which], device_id={"radius": other}, device_id_type=MESH,
        )

    left_copy = halo_copy(to_left, from_right, 0, jnp.maximum(me - 1, 0))
    right_copy = halo_copy(to_right, from_left, 1, jnp.minimum(me + 1, count - 1))

    chunk = (channels + extra_rows) // CHUNKS
    children = []
    for step in TREE:
        child = me + step
        mine = (lax.rem(me, 2 * step) == 0) if step < TREE[0] else (lax.rem(me, step) == 0)
        children.append((child, mine & (child < count)))

    def strip_copy(part, which):
        rows = pl.ds(part * chunk, chunk)
        return pltpu.make_async_remote_copy(
            src_ref=strip.at[rows, :], dst_ref=strip.at[rows, :],
            send_sem=strip_send.at[which, part], recv_sem=strip_recv.at[part],
            device_id={"radius": jnp.minimum(children[which][0], count - 1)}, device_id_type=MESH,
        )

    def send_on(part):
        for which in range(len(TREE)):
            @pl.when(children[which][1])
            def _():
                strip_copy(part, which).start()

    @pl.when(me == 0)
    def _():
        for part in range(CHUNKS):
            send_on(part)

    @pl.when(has_left)
    def _():
        left_copy.start()

    @pl.when(has_right)
    def _():
        right_copy.start()

    for copy in loads[2:]:
        copy.wait()
    build_coupling(channels, dipole, pattern, chan, square, joined, columns, lhs)

    @pl.when(me > 0)
    def _():
        for part in range(CHUNKS):
            strip_copy(part, 0).wait_recv()
            send_on(part)

    second = (lane >= 48) & (lane < 112)
    place = jnp.where(second, lax.rem(lane + 64, size), lane)
    in_right, in_left = place < HALO, place >= size - HALO
    in_strip = (place >= BASE) & (place < BASE + STRIP)
    here = me * size
    extra = jnp.where(in_right, here + size + place, jnp.where(in_left, here - size + place, place - BASE))
    valid = (in_right & has_right) | (in_left & has_left) | in_strip
    extra = jnp.where(valid, extra, 0)
    keep = jnp.where(valid, 1.0, 0.0).astype(F32)
    flip = jnp.where(second, -keep, keep)
    positions = jnp.concatenate([here + row_lane, here + lax.rem(row_lane + 64, size), extra[0:1, :]], axis=1)
    radial = inner_radius + (positions + 1).astype(F32) * spacing
    inverse = 1.0 / (radial * radial)

    @pl.when(has_right)
    def _():
        left_copy_in = halo_copy(to_left, from_right, 0, jnp.minimum(me + 1, count - 1))
        left_copy_in.wait_recv()

    @pl.when(jnp.logical_not(has_right))
    def _():
        from_right[...] = jnp.zeros_like(from_right)

    @pl.when(has_left)
    def _():
        right_copy_in = halo_copy(to_right, from_left, 1, jnp.maximum(me - 1, 0))
        right_copy_in.wait_recv()

    @pl.when(jnp.logical_not(has_left))
    def _():
        from_left[...] = jnp.zeros_like(from_left)

    def unpack(cut, pair):
        right, left, inner = from_right[cut, :], from_left[cut, :], strip[cut, :]
        if pair == 1:
            right, left = pltpu.roll(right, 96, 1), pltpu.roll(left, 32, 1)
        inner = pltpu.roll(inner, BASE if pair == 0 else BASE + 96, 1)
        found = jnp.where(in_right, right, jnp.where(in_left, left, inner))
        return jnp.where(valid, found, 0.0)

    def shift(value, amount):
        return pltpu.roll(value, amount % size, 1)

    def store_split(pair, start, tiles):
        for tile, value in enumerate(tiles):
            cols = slice((3 * pair + tile) * size, (3 * pair + tile + 1) * size)
            high, rest = halves(value)
            rhs[pl.ds(start, ROWS), cols] = high
            rhs[pl.ds(channels + start, ROWS), cols] = rest
            rhs[pl.ds(2 * channels + start, ROWS), cols] = high

    unit = 0.5 / (spacing * spacing) / 12.0
    prof_extra = unpack(slice(channels, channels + extra_rows), 0)
    prof_all = jnp.concatenate([padded_prof, turned_prof, prof_extra], axis=1)
    row = lax.broadcasted_iota(jnp.int32, (size, 1), 0)
    point = lax.rem(row, 64) - BASE
    def weights(values):
        found = jnp.zeros((size, 1), F32)
        for index, value in enumerate(values):
            found = jnp.where(point == index, value / unit, found)
        return found

    value_weight = weights((4.0, -6.0, 4.0, -1.0))
    slope_weight = weights((-13.0 / 3.0, 9.5, -7.0, 11.0 / 6.0))
    owner = jnp.concatenate([jnp.zeros((1, size), jnp.int32), jnp.ones((1, size), jnp.int32), jnp.where(second, 1, 0)[0:1, :]], axis=1)
    full = value_weight * prof_all[0:1, :] + slope_weight * prof_all[1:2, :]
    full = jnp.where((row // 64) == owner, full, 0.0)

    def chain(index):
        tile, at = index // size, lax.rem(index, size)
        half = lax.rem(at + 64, size)
        other = (at >= 48) & (at < 112)
        spot = jnp.where(other, half, at)
        place = jnp.where(spot < HALO, spot + size, jnp.where(spot >= size - HALO, spot - size, 1000 + spot))
        inside = (spot < BASE + STRIP) | (spot >= size - HALO)
        inside = inside & ((spot < HALO) | (spot >= BASE))
        place = jnp.where(inside, place + jnp.where(other, 4000, 0), 10000 + 10 * at)
        return jnp.where(tile == 0, at, jnp.where(tile == 1, 4000 + half, place))

    across = chain(lax.broadcasted_iota(jnp.int32, (1, 3 * size), 1))
    for tile in range(3):
        down = chain(row + tile * size)
        apart = jnp.abs(down - across)
        band = jnp.where(apart == 2, 1.0, jnp.where(apart == 1, -16.0, 0.0))
        if tile == 2:
            band = band + full
        high = band.astype(BF16)
        for copy in range(2):
            first = (3 * copy + tile) * size
            surface[first : first + size, :] = high
        if tile == 2:
            surface[6 * size :, :] = (band - high.astype(F32)).astype(BF16)

    rhs[3 * channels :, :] = jnp.zeros((rhs.shape[0] - 3 * channels, 6 * size), BF16)
    diagonal = 1.25 / (spacing * spacing) / unit

    def begin(start, carry):
        rows = pl.ds(start, ROWS)
        for tile in range(3):
            cols = slice(tile * size, (tile + 1) * size)
            level = columns[0, rows, :] + columns[1, rows, :] * inverse[:, cols]
            pot[rows, cols] = level / unit + diagonal
        for pair in range(2):
            tiles = [term[pair, rows, 0:size], term[pair, rows, size : 2 * size], unpack(rows, pair)]
            term[pair, rows, 2 * size :] = tiles[2]
            store_split(pair, start, tiles)
            total[0, pair, rows, :] = jnp.concatenate(tiles, axis=1)
            total[1, pair, rows, :] = jnp.zeros((ROWS, 3 * size), F32)
        return carry

    over_rows(begin)

    def grad_copy(other, slot):
        return pltpu.make_async_remote_copy(
            src_ref=partial, dst_ref=gathered.at[slot], send_sem=grad_send.at[other],
            recv_sem=grad_recv.at[slot], device_id={"radius": other}, device_id_type=MESH,
        )

    def one_step(step, _):
        strength = pulse[step]
        driven = (strength / unit) * radial

        def one_term(index, _):
            power = index + 1
            scale = unit * time_step / power.astype(F32)
            odd = lax.rem(power, 2)
            signed = jnp.where(odd == 1, -scale, scale)

            for block in range(3):
                cols = slice(block * 256, (block + 1) * 256)
                mixed[:, cols] = jnp.dot(lhs[0:channels, :], rhs[:, cols], preferred_element_type=F32)
            for pair in range(2):
                cols = slice(3 * pair * size, 3 * (pair + 1) * size)
                both = [rhs[0:channels, cols], rhs[channels : 2 * channels, cols], rhs[0:channels, cols.stop - size : cols.stop]]
                bound[pair] = jnp.dot(jnp.concatenate(both, axis=1), surface[...], preferred_element_type=F32)

            @pl.when(index == 0)
            def _():
                def meet(start, found):
                    rows = pl.ds(start, ROWS)
                    turned = shift(mixed[rows, size : 2 * size], 64) * term[1, rows, 0:size]
                    straight = shift(term[1, rows, size : 2 * size], 64) * mixed[rows, 0:size]
                    both = turned - straight
                    return found + both[0:8] + both[8:16]

                partial[step] = over_rows(meet, jnp.zeros((8, size), F32)) * radial[:, 0:size]

                @pl.when(step == STEPS - 1)
                def _():
                    def send(d, _):
                        grad_copy(lax.rem(me + d, count), me).start()
                        return 0

                    lax.fori_loop(1, count, send, 0)

            def advance(start, carry):
                rows = pl.ds(start, ROWS)
                for pair in range(2):
                    now = [term[pair, rows, t * size : (t + 1) * size] for t in range(3)]
                    new = []
                    for tile in range(3):
                        cols = slice(tile * size, (tile + 1) * size)
                        wide = slice((3 * pair + tile) * size, (3 * pair + tile + 1) * size)
                        value = bound[pair, rows, cols] + pot[rows, cols] * now[tile]
                        value = value + driven[:, cols] * mixed[rows, wide]
                        factor = (signed, -signed, signed * flip)[tile]
                        value = factor * value
                        new.append(value)
                        term[pair, rows, cols] = value
                        total[odd, pair, rows, cols] += value
                    store_split(pair, start, new)
                return carry

            over_rows(advance)
            return 0

        lax.fori_loop(0, ORDER, one_term, 0)

        def close(start, carry):
            rows = pl.ds(start, ROWS)
            for pair in range(2):
                tiles = []
                for tile in range(3):
                    cols = slice(tile * size, (tile + 1) * size)
                    source = (1, 0, 2)[tile]
                    turned = shift(total[1, pair, rows, source * size : (source + 1) * size], 64)
                    tiles.append(total[0, pair, rows, cols] + turned)
                for tile in range(3):
                    cols = slice(tile * size, (tile + 1) * size)
                    term[pair, rows, cols] = tiles[tile]
                    total[0, pair, rows, cols] = tiles[tile]
                    total[1, pair, rows, cols] = jnp.zeros((ROWS, size), F32)
                store_split(pair, start, tiles)
            return carry

        over_rows(close)
        return 0

    lax.fori_loop(0, STEPS, one_step, 0)

    def finish_rows(start, carry):
        rows = pl.ds(start, ROWS)
        for pair in range(2):
            out[2 * pair, rows, :] = term[pair, rows, 0:size]
            out[2 * pair + 1, rows, :] = shift(term[pair, rows, size : 2 * size], 64)
        return carry

    over_rows(finish_rows)

    gathered[me] = partial[...]

    def collect(d, _):
        other = lax.rem(me + d, count)
        copy = grad_copy(other, other)
        copy.wait_recv()
        return 0

    lax.fori_loop(1, count, collect, 0)
    normalizer = math.sqrt(channels * count * size) * (inner_radius + count * size * spacing)
    for step in range(STEPS):
        found = jnp.zeros((8, size), F32)
        for index in range(count):
            found = found + gathered[index, step]
        grad[step] = jnp.sum(found) / normalizer

    def finish(d, _):
        grad_copy(lax.rem(me + d, count), me).wait_send()
        return 0

    lax.fori_loop(1, count, finish, 0)

    @pl.when(has_left)
    def _():
        left_copy.wait_send()

    @pl.when(has_right)
    def _():
        right_copy.wait_send()

    for which in range(len(TREE)):
        @pl.when(children[which][1])
        def _():
            for part in range(CHUNKS):
                strip_copy(part, which).wait_send()


def per_device(count, states, dipole, pattern, angular, thresholds, surface_profile, pulse_field):
    channels = states.shape[1]
    size = states.shape[2]
    padded = -(-channels // BLOCK) * BLOCK
    depth = -(-3 * channels // 256) * 256
    fill = (0, padded - channels)
    chan = jnp.stack([jnp.pad(angular.astype(F32), fill), jnp.pad(thresholds, fill)]).reshape(-1, BLOCK)
    vmem = pl.BlockSpec(memory_space=pltpu.VMEM)
    smem = pl.BlockSpec(memory_space=pltpu.SMEM)
    message = pltpu.VMEM((channels + 16, size), F32)
    wide = (2, channels, 3 * size)
    return pl.pallas_call(
        functools.partial(kernel, count, channels),
        out_shape=(
            jax.ShapeDtypeStruct(states.shape, F32),
            jax.ShapeDtypeStruct(pulse_field.shape, F32),
        ),
        in_specs=[pl.BlockSpec(memory_space=pl.ANY)] * 5 + [smem],
        out_specs=(vmem, smem),
        scratch_shapes=[
            message, message, message, message, message,
            pltpu.VMEM(wide, F32),
            pltpu.VMEM((2,) + wide, F32),
            pltpu.VMEM((depth, 6 * size), BF16),
            pltpu.VMEM((channels, 6 * size), F32),
            pltpu.VMEM(wide, F32),
            pltpu.VMEM((7 * size, 3 * size), BF16),
            pltpu.VMEM((channels, 3 * size), F32),
            pltpu.VMEM((STEPS, 8, size), F32),
            pltpu.VMEM((count, STEPS, 8, size), F32),
            pltpu.VMEM((padded, depth), BF16),
            pltpu.VMEM((padded, padded), F32),
            pltpu.VMEM((BLOCK, BLOCK), F32),
            pltpu.VMEM((2, padded, BLOCK), F32),
            pltpu.VMEM(states.shape, F32),
            pltpu.VMEM(dipole.shape, F32),
            pltpu.VMEM(pattern.shape, jnp.int32),
            pltpu.VMEM(chan.shape, F32),
            pltpu.VMEM(surface_profile.shape, F32),
            pltpu.SemaphoreType.DMA((5,)),
            pltpu.SemaphoreType.DMA((2,)),
            pltpu.SemaphoreType.DMA((2,)),
            pltpu.SemaphoreType.DMA((len(TREE), CHUNKS)),
            pltpu.SemaphoreType.DMA((CHUNKS,)),
            pltpu.SemaphoreType.DMA((count,)),
            pltpu.SemaphoreType.DMA((count,)),
        ],
        compiler_params=pltpu.CompilerParams(
            collective_id=0, has_side_effects=True, vmem_limit_bytes=48 * 1024 * 1024
        ),
        cost_estimate=pl.CostEstimate(flops=8000000000, bytes_accessed=4000000, transcendentals=0),
    )(states, dipole, pattern, chan, surface_profile, pulse_field)


def solution(mesh):
    return jax.shard_map(
        functools.partial(per_device, mesh.shape["radius"]),
        mesh=mesh,
        in_specs=(P("groups", None, "radius"), P(), P(), P(), P(), P(None, "radius"), P("groups")),
        out_specs=(P("groups", None, "radius"), P("groups")),
        check_vma=False,
    )
```

```python
import functools
import math

import jax
import jax.numpy as jnp
from jax import lax
from jax.experimental import pallas as pl
from jax.experimental.pallas import tpu as pltpu
from jax.sharding import PartitionSpec as P

STEPS = 2
ORDER = 4
inner_radius = 20.0
spacing = 0.08
time_step = 0.005

HALO = 2 * ORDER * STEPS
STRIP = HALO + 2
BASE = 20
ROWS = 16
CHUNKS = 13
BLOCK = 128
AGAIN = 18
GROUP = 5
TREE = (4, 2, 1)
MESH = pl.DeviceIdType.MESH
F32 = jnp.float32
BF16 = jnp.bfloat16


def halves(value):
    high = value.astype(BF16)
    return high, (value - high.astype(F32)).astype(BF16)


def build_coupling(channels, dipole, pattern, chan, square, joined, columns, lhs):
    blocks = pattern.shape[0]
    parts = square.shape[0] // BLOCK
    owned = channels // blocks
    square[...] = jnp.zeros_like(square)
    square[0:channels, 0:channels] = dipole[...]
    joined[...] = jnp.zeros_like(joined)
    joined[0:blocks, 0:blocks] = pattern[...].astype(F32)
    either = jnp.maximum(joined[...], joined[...].T).astype(BF16)
    lane = lax.broadcasted_iota(jnp.int32, (BLOCK, BLOCK), 1)
    row = lax.broadcasted_iota(jnp.int32, (BLOCK, BLOCK), 0)

    def pick(part):
        return jnp.where((row + part * BLOCK) // owned == lane, 1.0, 0.0).astype(BF16)

    def spread(which, part):
        return jnp.broadcast_to(chan[which : which + 1, part * BLOCK : (part + 1) * BLOCK], (BLOCK, BLOCK))

    across = [spread(0, part) for part in range(parts)]
    picks = [pick(part) for part in range(parts)]
    for i in range(parts):
        down = across[i].T
        rows = slice(i * BLOCK, (i + 1) * BLOCK)
        columns[0, rows, :] = spread(1, i).T
        columns[1, rows, :] = 0.5 * (down * (down + 1.0))
        held = jnp.dot(picks[i], either, preferred_element_type=F32).astype(BF16)
        found = {}
        for j in range(parts):
            cols = slice(j * BLOCK, (j + 1) * BLOCK)
            mask = lax.dot_general(held, picks[j], (((1,), (1,)), ((), ())), preferred_element_type=F32)
            allowed = (mask > 0.5) & (jnp.abs(down - across[j]) == 1.0)
            mean = 0.5 * (square[rows, cols] + square[cols, rows].T)
            coupling = jnp.where(allowed, mean, 0.0)
            high = coupling.astype(BF16).astype(F32)
            rest = coupling - high
            for copy, value in enumerate((high, high, rest)):
                place = copy * channels + j * BLOCK
                tile, off = place // BLOCK, place % BLOCK
                moved = pltpu.roll(value, off, 1) if off else value
                for tile, kept in ((tile, lane >= off), (tile + 1, lane < off)):
                    if tile in found:
                        found[tile] = found[tile] + jnp.where(kept, moved, 0.0)
                    elif tile < lhs.shape[1] // BLOCK:
                        found[tile] = jnp.where(kept, moved, 0.0)
        for tile, value in found.items():
            lhs[rows, tile * BLOCK : (tile + 1) * BLOCK] = value.astype(BF16)


def kernel(
    count, channels, states_in, dipole_in, pattern_in, angular_in, thresholds_in, prof_in, pulse, out, grad,
    to_left, to_right, from_left, from_right, strip,
    term, total, rhs, mixed, bound, surface, pot, partial, gathered,
    lhs, square, joined, columns, states, dipole, pattern, angular, thresholds, chan, prof, load,
    halo_send, halo_recv, strip_send, strip_recv, grad_send, grad_recv,
):
    me = lax.axis_index("radius")
    size = 128
    has_left, has_right = me > 0, me < count - 1
    lane = lax.broadcasted_iota(jnp.int32, (ROWS, size), 1)
    row_lane = lane[0:1, :]
    extra_rows = 16
    loads = [
        pltpu.make_async_copy(source, target, load.at[which])
        for which, (source, target) in enumerate(
            ((states_in, states), (prof_in, prof), (dipole_in, dipole), (pattern_in, pattern), (angular_in, angular), (thresholds_in, thresholds))
        )
    ]
    for copy in loads:
        copy.start()

    def over_rows(body, carry=0):
        def several(index, carry):
            for part in range(GROUP):
                carry = body(pl.multiple_of((index * GROUP + part) * ROWS, ROWS), carry)
            return carry

        return lax.fori_loop(0, channels // ROWS // GROUP, several, carry)

    barrier = pltpu.get_barrier_semaphore()

    def greet(d, _):
        other = lax.rem(me + d, count)
        pl.semaphore_signal(barrier, inc=1, device_id={"radius": other}, device_id_type=MESH)
        return 0

    lax.fori_loop(1, count, greet, 0)

    loads[0].wait()
    loads[1].wait()
    low = lane < 64
    low_quarter = lax.rem(lane, 64) < 32
    padded_prof = jnp.concatenate([prof[...], jnp.zeros((extra_rows - 2, size), F32)], axis=0)
    turned_prof = pltpu.roll(padded_prof, 64, 1)

    def pack(rows, parts):
        a, b, c, d = parts
        left = jnp.where(low_quarter, jnp.where(low, a, b), pltpu.roll(jnp.where(low, c, d), 32, 1))
        right = jnp.where(low_quarter, pltpu.roll(jnp.where(low, d, c), 96, 1), jnp.where(low, b, a))
        to_left[rows, :] = left
        to_right[rows, :] = right

    def pack_rows(start, carry):
        rows = pl.ds(start, ROWS)
        a, c = states[0, rows, :], states[2, rows, :]
        b, d = pltpu.roll(states[1, rows, :], 64, 1), pltpu.roll(states[3, rows, :], 64, 1)
        pack(rows, (a, b, c, d))
        for pair, (first, other) in enumerate(((a, b), (c, d))):
            term[pair, rows, 0:size] = first
            term[pair, rows, size : 2 * size] = other
        return carry

    over_rows(pack_rows)
    pack(slice(channels, channels + extra_rows), (padded_prof, turned_prof, padded_prof, turned_prof))

    @pl.when(me == 0)
    def _():
        strip[...] = to_left[...]

    pl.semaphore_wait(barrier, count - 1)

    def halo_copy(source, target, which, other):
        return pltpu.make_async_remote_copy(
            src_ref=source, dst_ref=target, send_sem=halo_send.at[which],
            recv_sem=halo_recv.at[which], device_id={"radius": other}, device_id_type=MESH,
        )

    left_copy = halo_copy(to_left, from_right, 0, jnp.maximum(me - 1, 0))
    right_copy = halo_copy(to_right, from_left, 1, jnp.minimum(me + 1, count - 1))

    chunk = (channels + extra_rows) // CHUNKS
    children = []
    for step in TREE:
        child = me + step
        mine = (lax.rem(me, 2 * step) == 0) if step < TREE[0] else (lax.rem(me, step) == 0)
        children.append((child, mine & (child < count)))

    def strip_copy(part, which):
        rows = pl.ds(part * chunk, chunk)
        return pltpu.make_async_remote_copy(
            src_ref=strip.at[rows, :], dst_ref=strip.at[rows, :],
            send_sem=strip_send.at[which, part], recv_sem=strip_recv.at[part],
            device_id={"radius": jnp.minimum(children[which][0], count - 1)}, device_id_type=MESH,
        )

    def send_on(part):
        for which in range(len(TREE)):
            @pl.when(children[which][1])
            def _():
                strip_copy(part, which).start()

    @pl.when(me == 0)
    def _():
        for part in range(CHUNKS):
            send_on(part)

    @pl.when(has_left)
    def _():
        left_copy.start()

    @pl.when(has_right)
    def _():
        right_copy.start()

    for copy in loads[2:]:
        copy.wait()
    chan[...] = jnp.zeros_like(chan)
    chan[0:1, 0:channels] = angular[...].astype(F32)
    chan[1:2, 0:channels] = thresholds[...]
    build_coupling(channels, dipole, pattern, chan, square, joined, columns, lhs)

    @pl.when(me > 0)
    def _():
        for part in range(CHUNKS):
            strip_copy(part, 0).wait_recv()
            send_on(part)

    second = (lane >= 48) & (lane < 112)
    place = jnp.where(second, lax.rem(lane + 64, size), lane)
    in_right, in_left = place < HALO, place >= size - HALO
    in_strip = (place >= BASE) & (place < BASE + STRIP)
    here = me * size
    extra = jnp.where(in_right, here + size + place, jnp.where(in_left, here - size + place, place - BASE))
    valid = (in_right & has_right) | (in_left & has_left) | in_strip
    extra = jnp.where(valid, extra, 0)
    keep = jnp.where(valid, 1.0, 0.0).astype(F32)
    flip = jnp.where(second, -keep, keep)
    positions = jnp.concatenate([here + row_lane, here + lax.rem(row_lane + 64, size), extra[0:1, :]], axis=1)
    radial = inner_radius + (positions + 1).astype(F32) * spacing
    inverse = 1.0 / (radial * radial)

    @pl.when(has_right)
    def _():
        left_copy_in = halo_copy(to_left, from_right, 0, jnp.minimum(me + 1, count - 1))
        left_copy_in.wait_recv()

    @pl.when(jnp.logical_not(has_right))
    def _():
        from_right[...] = jnp.zeros_like(from_right)

    @pl.when(has_left)
    def _():
        right_copy_in = halo_copy(to_right, from_left, 1, jnp.maximum(me - 1, 0))
        right_copy_in.wait_recv()

    @pl.when(jnp.logical_not(has_left))
    def _():
        from_left[...] = jnp.zeros_like(from_left)

    def unpack(cut, pair):
        right, left, inner = from_right[cut, :], from_left[cut, :], strip[cut, :]
        if pair == 1:
            right, left = pltpu.roll(right, 96, 1), pltpu.roll(left, 32, 1)
        inner = pltpu.roll(inner, BASE if pair == 0 else BASE + 96, 1)
        found = jnp.where(in_right, right, jnp.where(in_left, left, inner))
        return jnp.where(valid, found, 0.0)

    def shift(value, amount):
        return pltpu.roll(value, amount % size, 1)

    def wide(pair, tile):
        first = 4 * size + pair * size if tile == 2 else 2 * pair * size + tile * size
        return slice(first, first + size)

    near = (lax.rem(lane, 64) >= BASE) & (lax.rem(lane, 64) < BASE + 4)

    def store_tile(pair, tile, start, value):
        cols = wide(pair, tile)
        high, rest = halves(value)
        if tile == 2:
            again = pltpu.roll(jnp.where(near, high.astype(F32), 0.0), AGAIN, 1)
            high = (high.astype(F32) + again).astype(BF16)
        rhs[pl.ds(start, ROWS), cols] = high
        rhs[pl.ds(channels + start, ROWS), cols] = rest
        rhs[pl.ds(2 * channels + start, ROWS), cols] = high

    def store_split(pair, start, tiles):
        for tile, value in enumerate(tiles):
            store_tile(pair, tile, start, value)

    unit = 0.5 / (spacing * spacing) / 12.0
    prof_extra = unpack(slice(channels, channels + extra_rows), 0)
    prof_all = jnp.concatenate([padded_prof, turned_prof, prof_extra], axis=1)
    row = lax.broadcasted_iota(jnp.int32, (size, 1), 0)
    spot = lax.rem(row, 64)
    again = (spot >= BASE + AGAIN) & (spot < BASE + AGAIN + 4)
    point = spot - BASE
    def weights(values):
        found = jnp.zeros((size, 1), F32)
        for index, value in enumerate(values):
            found = jnp.where(point == index, value / unit, found)
        return found

    value_weight = weights((4.0, -6.0, 4.0, -1.0))
    slope_weight = weights((-13.0 / 3.0, 9.5, -7.0, 11.0 / 6.0))
    owner = jnp.concatenate([jnp.zeros((1, size), jnp.int32), jnp.ones((1, size), jnp.int32), jnp.where(second, 1, 0)[0:1, :]], axis=1)
    full = value_weight * prof_all[0:1, :] + slope_weight * prof_all[1:2, :]
    full = jnp.where((row // 64) == owner, full, 0.0)

    def chain(index):
        tile, at = index // size, lax.rem(index, size)
        half = lax.rem(at + 64, size)
        other = (at >= 48) & (at < 112)
        spot = jnp.where(other, half, at)
        place = jnp.where(spot < HALO, spot + size, jnp.where(spot >= size - HALO, spot - size, 1000 + spot))
        inside = (spot < BASE + STRIP) | (spot >= size - HALO)
        inside = inside & ((spot < HALO) | (spot >= BASE))
        place = jnp.where(inside, place + jnp.where(other, 4000, 0), 10000 + 10 * at)
        return jnp.where(tile == 0, at, jnp.where(tile == 1, 4000 + half, place))

    across = chain(lax.broadcasted_iota(jnp.int32, (1, 3 * size), 1))
    for tile in range(3):
        down = chain(row + tile * size)
        apart = jnp.abs(down - across)
        band = jnp.where(apart == 2, 1.0, jnp.where(apart == 1, -16.0, 0.0))
        if tile == 2:
            band = band + full
        high = band.astype(BF16)
        if tile == 2:
            low_part = pltpu.roll(band - high.astype(F32), AGAIN, 0)
            high = jnp.where(again, low_part, high.astype(F32)).astype(BF16)
        for copy in range(2):
            first = (3 * copy + tile) * size
            surface[first : first + size, :] = high

    rhs[3 * channels :, :] = jnp.zeros((rhs.shape[0] - 3 * channels, 6 * size), BF16)
    diagonal = 1.25 / (spacing * spacing) / unit

    def begin(start, carry):
        rows = pl.ds(start, ROWS)
        for tile in range(3):
            cols = slice(tile * size, (tile + 1) * size)
            level = columns[0, rows, :] + columns[1, rows, :] * inverse[:, cols]
            pot[rows, cols] = level / unit + diagonal
        for pair in range(2):
            tiles = [term[pair, rows, 0:size], term[pair, rows, size : 2 * size], unpack(rows, pair)]
            term[pair, rows, 2 * size :] = tiles[2]
            store_split(pair, start, tiles)
            total[0, pair, rows, :] = jnp.concatenate(tiles, axis=1)
            total[1, pair, rows, :] = jnp.zeros((ROWS, 3 * size), F32)
        return carry

    over_rows(begin)

    def grad_copy(other, slot):
        return pltpu.make_async_remote_copy(
            src_ref=partial, dst_ref=gathered.at[slot], send_sem=grad_send.at[other],
            recv_sem=grad_recv.at[slot], device_id={"radius": other}, device_id_type=MESH,
        )

    def one_step(step, _):
        strength = pulse[step]
        driven = (strength / unit) * radial

        def one_term(index, _):
            power = index + 1
            scale = unit * time_step / power.astype(F32)
            odd = lax.rem(power, 2)
            signed = jnp.where(odd == 1, -scale, scale)

            stacked = []
            for pair in range(2):
                tiles = [rhs[part : part + channels, wide(pair, tile)] for part in (0, channels) for tile in range(3)]
                stacked.append(jnp.concatenate(tiles, axis=1))
            bound[...] = jnp.dot(jnp.concatenate(stacked, axis=0), surface[...], preferred_element_type=F32)

            def mix(block):
                cols = slice(block * 2 * size, (block + 1) * 2 * size)
                mixed[:, cols] = jnp.dot(lhs[0:channels, :], rhs[:, cols], preferred_element_type=F32)

            mix(0)

            @pl.when(index == 0)
            def _():
                def meet(start, found):
                    rows = pl.ds(start, ROWS)
                    turned = shift(mixed[rows, size : 2 * size], 64) * term[1, rows, 0:size]
                    straight = shift(term[1, rows, size : 2 * size], 64) * mixed[rows, 0:size]
                    both = turned - straight
                    return found + both[0:8] + both[8:16]

                partial[step] = over_rows(meet, jnp.zeros((8, size), F32)) * radial[:, 0:size]

                @pl.when(step == STEPS - 1)
                def _():
                    def send(d, _):
                        grad_copy(lax.rem(me + d, count), me).start()
                        return 0

                    lax.fori_loop(1, count, send, 0)

            def advance(pair, tile):
                cols = slice(tile * size, (tile + 1) * size)
                factor = (signed, -signed, signed * flip)[tile]
                spread_driven = jnp.broadcast_to(driven[:, cols], (ROWS, size))
                for start in range(0, channels, ROWS):
                    rows = slice(start, start + ROWS)
                    value = bound[pair * channels + start : pair * channels + start + ROWS, cols]
                    value = value + pot[rows, cols] * term[pair, rows, cols]
                    value = value + spread_driven * mixed[rows, wide(pair, tile)]
                    value = factor * value
                    term[pair, rows, cols] = value
                    total[odd, pair, rows, cols] += value
                    store_tile(pair, tile, start, value)

            mix(1)
            advance(0, 0)
            advance(0, 1)
            mix(2)
            advance(1, 0)
            advance(1, 1)
            advance(0, 2)
            advance(1, 2)
            return 0

        lax.fori_loop(0, ORDER, one_term, 0)

        def close(start, carry):
            rows = pl.ds(start, ROWS)
            for pair in range(2):
                tiles = []
                for tile in range(3):
                    cols = slice(tile * size, (tile + 1) * size)
                    source = (1, 0, 2)[tile]
                    turned = shift(total[1, pair, rows, source * size : (source + 1) * size], 64)
                    tiles.append(total[0, pair, rows, cols] + turned)
                for tile in range(3):
                    cols = slice(tile * size, (tile + 1) * size)
                    term[pair, rows, cols] = tiles[tile]
                    total[0, pair, rows, cols] = tiles[tile]
                    total[1, pair, rows, cols] = jnp.zeros((ROWS, size), F32)
                store_split(pair, start, tiles)
            return carry

        over_rows(close)
        return 0

    lax.fori_loop(0, STEPS, one_step, 0)

    def finish_rows(start, carry):
        rows = pl.ds(start, ROWS)
        for pair in range(2):
            out[2 * pair, rows, :] = term[pair, rows, 0:size]
            out[2 * pair + 1, rows, :] = shift(term[pair, rows, size : 2 * size], 64)
        return carry

    over_rows(finish_rows)

    gathered[me] = partial[...]

    def collect(d, _):
        other = lax.rem(me + d, count)
        copy = grad_copy(other, other)
        copy.wait_recv()
        return 0

    lax.fori_loop(1, count, collect, 0)
    normalizer = math.sqrt(channels * count * size) * (inner_radius + count * size * spacing)
    for step in range(STEPS):
        found = jnp.zeros((8, size), F32)
        for index in range(count):
            found = found + gathered[index, step]
        grad[step] = jnp.sum(found) / normalizer

    def finish(d, _):
        grad_copy(lax.rem(me + d, count), me).wait_send()
        return 0

    lax.fori_loop(1, count, finish, 0)

    @pl.when(has_left)
    def _():
        left_copy.wait_send()

    @pl.when(has_right)
    def _():
        right_copy.wait_send()

    for which in range(len(TREE)):
        @pl.when(children[which][1])
        def _():
            for part in range(CHUNKS):
                strip_copy(part, which).wait_send()


def per_device(count, states, dipole, pattern, angular, thresholds, surface_profile, pulse_field):
    channels = states.shape[1]
    size = states.shape[2]
    padded = -(-channels // BLOCK) * BLOCK
    depth = -(-3 * channels // 256) * 256
    angular, thresholds = angular[None, :], thresholds[None, :]
    vmem = pl.BlockSpec(memory_space=pltpu.VMEM)
    smem = pl.BlockSpec(memory_space=pltpu.SMEM)
    message = pltpu.VMEM((channels + 16, size), F32)
    wide = (2, channels, 3 * size)
    return pl.pallas_call(
        functools.partial(kernel, count, channels),
        out_shape=(
            jax.ShapeDtypeStruct(states.shape, F32),
            jax.ShapeDtypeStruct(pulse_field.shape, F32),
        ),
        in_specs=[pl.BlockSpec(memory_space=pl.ANY)] * 6 + [smem],
        out_specs=(vmem, smem),
        scratch_shapes=[
            message, message, message, message, message,
            pltpu.VMEM(wide, F32),
            pltpu.VMEM((2,) + wide, F32),
            pltpu.VMEM((depth, 6 * size), BF16),
            pltpu.VMEM((channels, 6 * size), F32),
            pltpu.VMEM((2 * channels, 3 * size), F32),
            pltpu.VMEM((6 * size, 3 * size), BF16),
            pltpu.VMEM((channels, 3 * size), F32),
            pltpu.VMEM((STEPS, 8, size), F32),
            pltpu.VMEM((count, STEPS, 8, size), F32),
            pltpu.VMEM((padded, depth), BF16),
            pltpu.VMEM((padded, padded), F32),
            pltpu.VMEM((BLOCK, BLOCK), F32),
            pltpu.VMEM((2, padded, BLOCK), F32),
            pltpu.VMEM(states.shape, F32),
            pltpu.VMEM(dipole.shape, F32),
            pltpu.VMEM(pattern.shape, jnp.int32),
            pltpu.VMEM(angular.shape, jnp.int32),
            pltpu.VMEM(thresholds.shape, F32),
            pltpu.VMEM((8, padded), F32),
            pltpu.VMEM(surface_profile.shape, F32),
            pltpu.SemaphoreType.DMA((6,)),
            pltpu.SemaphoreType.DMA((2,)),
            pltpu.SemaphoreType.DMA((2,)),
            pltpu.SemaphoreType.DMA((len(TREE), CHUNKS)),
            pltpu.SemaphoreType.DMA((CHUNKS,)),
            pltpu.SemaphoreType.DMA((count,)),
            pltpu.SemaphoreType.DMA((count,)),
        ],
        compiler_params=pltpu.CompilerParams(
            collective_id=0, has_side_effects=True, vmem_limit_bytes=63 * 1024 * 1024
        ),
        cost_estimate=pl.CostEstimate(flops=8000000000, bytes_accessed=4000000, transcendentals=0),
    )(states, dipole, pattern, angular, thresholds, surface_profile, pulse_field)


def solution(mesh):
    return jax.shard_map(
        functools.partial(per_device, mesh.shape["radius"]),
        mesh=mesh,
        in_specs=(P("groups", None, "radius"), P(), P(), P(), P(), P(None, "radius"), P("groups")),
        out_specs=(P("groups", None, "radius"), P("groups")),
        check_vma=False,
    )
```

```python
import functools
import math

import jax
import jax.numpy as jnp
from jax import lax
from jax.experimental import pallas as pl
from jax.experimental.pallas import tpu as pltpu
from jax.sharding import PartitionSpec as P

STEPS = 2
ORDER = 4
inner_radius = 20.0
spacing = 0.08
time_step = 0.005

HALO = 2 * ORDER * STEPS
STRIP = HALO + 2
BASE = 20
ROWS = 16
CHUNKS = 4
BLOCK = 128
AGAIN = 18
GROUP = 5
TREE = (4, 2, 1)
MESH = pl.DeviceIdType.MESH
F32 = jnp.float32
BF16 = jnp.bfloat16


def halves(value):
    high = value.astype(BF16)
    return high, (value - high.astype(F32)).astype(BF16)


def build_coupling(channels, dipole, pattern, chan, square, joined, columns, lhs):
    blocks = pattern.shape[0]
    parts = square.shape[0] // BLOCK
    owned = channels // blocks
    square[...] = jnp.zeros_like(square)
    square[0:channels, 0:channels] = dipole[...]
    joined[...] = jnp.zeros_like(joined)
    joined[0:blocks, 0:blocks] = pattern[...].astype(F32)
    either = jnp.maximum(joined[...], joined[...].T).astype(BF16)
    lane = lax.broadcasted_iota(jnp.int32, (BLOCK, BLOCK), 1)
    row = lax.broadcasted_iota(jnp.int32, (BLOCK, BLOCK), 0)

    def pick(place, block):
        first = block * owned
        return jnp.where((place >= first) & (place < first + owned), 1.0, 0.0).astype(BF16)

    def spread(which, part):
        return jnp.broadcast_to(chan[which : which + 1, part * BLOCK : (part + 1) * BLOCK], (BLOCK, BLOCK))

    across = [spread(0, part) for part in range(parts)]
    picks = pick(
        lax.broadcasted_iota(jnp.int32, (BLOCK, parts * BLOCK), 1),
        lax.broadcasted_iota(jnp.int32, (BLOCK, parts * BLOCK), 0),
    )
    for i in range(parts):
        down = across[i].T
        rows = slice(i * BLOCK, (i + 1) * BLOCK)
        columns[0, rows, :] = spread(1, i).T
        columns[1, rows, :] = 0.5 * (down * (down + 1.0))
        held = jnp.dot(pick(row + i * BLOCK, lane), either, preferred_element_type=F32).astype(BF16)
        masks = jnp.dot(held, picks, preferred_element_type=F32)
        found = {}
        for j in range(parts):
            cols = slice(j * BLOCK, (j + 1) * BLOCK)
            allowed = (masks[:, cols] > 0.5) & (jnp.abs(down - across[j]) == 1.0)
            mean = 0.5 * (square[rows, cols] + square[cols, rows].T)
            coupling = jnp.where(allowed, mean, 0.0)
            high = coupling.astype(BF16).astype(F32)
            rest = coupling - high
            for copy, value in enumerate((high, high, rest)):
                place = copy * channels + j * BLOCK
                tile, off = place // BLOCK, place % BLOCK
                moved = pltpu.roll(value, off, 1) if off else value
                for tile, kept in ((tile, lane >= off), (tile + 1, lane < off)):
                    if tile in found:
                        found[tile] = found[tile] + jnp.where(kept, moved, 0.0)
                    elif tile < lhs.shape[1] // BLOCK:
                        found[tile] = jnp.where(kept, moved, 0.0)
        for tile, value in found.items():
            lhs[rows, tile * BLOCK : (tile + 1) * BLOCK] = value.astype(BF16)


def kernel(
    count, channels, states_in, dipole_in, pattern_in, angular_in, thresholds_in, prof_in, pulse, out, grad,
    to_left, to_right, from_left, from_right, strip, left_half, right_half, left_in, right_in,
    term, total, rhs, mixed, bound, surface, pot, partial, gathered,
    lhs, square, joined, columns, states, dipole, pattern, angular, thresholds, chan, prof, load,
    halo_send, halo_recv, strip_send, strip_recv, grad_send, grad_recv,
):
    me = lax.axis_index("radius")
    size = 128
    has_left, has_right = me > 0, me < count - 1
    lane = lax.broadcasted_iota(jnp.int32, (ROWS, size), 1)
    row_lane = lane[0:1, :]
    extra_rows = 16
    loads = [
        pltpu.make_async_copy(source, target, load.at[which])
        for which, (source, target) in enumerate(
            ((states_in, states), (prof_in, prof), (dipole_in, dipole), (pattern_in, pattern), (angular_in, angular), (thresholds_in, thresholds))
        )
    ]
    for copy in loads:
        copy.start()

    def over_rows(body, carry=0):
        def several(index, carry):
            for part in range(GROUP):
                carry = body(pl.multiple_of((index * GROUP + part) * ROWS, ROWS), carry)
            return carry

        return lax.fori_loop(0, channels // ROWS // GROUP, several, carry)

    barrier = pltpu.get_barrier_semaphore()

    def greet(d, _):
        other = lax.rem(me + d, count)
        pl.semaphore_signal(barrier, inc=1, device_id={"radius": other}, device_id_type=MESH)
        return 0

    lax.fori_loop(1, count, greet, 0)

    loads[0].wait()
    loads[1].wait()
    low = lane < 64
    low_quarter = (lane & 63) < 32
    padded_prof = jnp.concatenate([prof[...], jnp.zeros((extra_rows - 2, size), F32)], axis=0)
    turned_prof = pltpu.roll(padded_prof, 64, 1)

    def pack(rows, parts):
        a, b, c, d = parts
        left = jnp.where(low_quarter, jnp.where(low, a, b), pltpu.roll(jnp.where(low, c, d), 32, 1))
        right = jnp.where(low_quarter, pltpu.roll(jnp.where(low, d, c), 96, 1), jnp.where(low, b, a))
        to_left[rows, :] = left
        to_right[rows, :] = right

    def pack_rows(start, carry):
        rows = pl.ds(start, ROWS)
        a, c = states[0, rows, :], states[2, rows, :]
        b, d = pltpu.roll(states[1, rows, :], 64, 1), pltpu.roll(states[3, rows, :], 64, 1)
        pack(rows, (a, b, c, d))
        for pair, (first, other) in enumerate(((a, b), (c, d))):
            term[pair, rows, 0:size] = first
            term[pair, rows, size : 2 * size] = other
        return carry

    over_rows(pack_rows)
    pack(slice(channels, channels + extra_rows), (padded_prof, turned_prof, padded_prof, turned_prof))

    @pl.when(me == 0)
    def _():
        strip[...] = to_left[...]

    message = (channels + extra_rows) // 2
    first_half = (lane & 31) < HALO

    def squeeze(index, _):
        near_rows = pl.ds(pl.multiple_of(index * ROWS, ROWS), ROWS)
        far_rows = pl.ds(pl.multiple_of(message + index * ROWS, ROWS), ROWS)
        left_half[near_rows, :] = jnp.where(first_half, to_left[near_rows, :], pltpu.roll(to_left[far_rows, :], HALO, 1))
        right_half[near_rows, :] = jnp.where(
            first_half, pltpu.roll(to_right[far_rows, :], size - HALO, 1), to_right[near_rows, :]
        )
        return 0

    lax.fori_loop(0, message // ROWS, squeeze, 0)

    pl.semaphore_wait(barrier, count - 1)

    def halo_copy(source, target, which, other):
        return pltpu.make_async_remote_copy(
            src_ref=source, dst_ref=target, send_sem=halo_send.at[which],
            recv_sem=halo_recv.at[which], device_id={"radius": other}, device_id_type=MESH,
        )

    left_copy = halo_copy(left_half, right_in, 0, jnp.maximum(me - 1, 0))
    right_copy = halo_copy(right_half, left_in, 1, jnp.minimum(me + 1, count - 1))

    chunk = (channels + extra_rows) // CHUNKS
    children = []
    for step in TREE:
        child = me + step
        mine = (lax.rem(me, 2 * step) == 0) if step < TREE[0] else (lax.rem(me, step) == 0)
        children.append((child, mine & (child < count)))

    def strip_copy(part, which):
        rows = pl.ds(part * chunk, chunk)
        return pltpu.make_async_remote_copy(
            src_ref=strip.at[rows, :], dst_ref=strip.at[rows, :],
            send_sem=strip_send.at[which, part], recv_sem=strip_recv.at[part],
            device_id={"radius": jnp.minimum(children[which][0], count - 1)}, device_id_type=MESH,
        )

    def send_on(part):
        for which in range(len(TREE)):
            @pl.when(children[which][1])
            def _():
                strip_copy(part, which).start()

    @pl.when(me == 0)
    def _():
        for part in range(CHUNKS):
            send_on(part)

    @pl.when(has_left)
    def _():
        left_copy.start()

    @pl.when(has_right)
    def _():
        right_copy.start()

    for copy in loads[2:]:
        copy.wait()
    chan[...] = jnp.zeros_like(chan)
    chan[0:1, 0:channels] = angular[...].astype(F32)
    chan[1:2, 0:channels] = thresholds[...]
    pass_first = (lax.rem(me, TREE[0]) == 0) & (me > 0) & (me <= count // 2)
    build_phase = jnp.where(pass_first, 1, 0)

    def phase(which, _):
        @pl.when(which == build_phase)
        def _():
            build_coupling(channels, dipole, pattern, chan, square, joined, columns, lhs)

        @pl.when((which != build_phase) & (me > 0))
        def _():
            for part in range(CHUNKS):
                strip_copy(part, 0).wait_recv()
                send_on(part)

        return 0

    lax.fori_loop(0, 2, phase, 0)

    second = (lane >= 48) & (lane < 112)
    place = jnp.where(second, ((lane + 64) & (size - 1)), lane)
    in_right, in_left = place < HALO, place >= size - HALO
    in_strip = (place >= BASE) & (place < BASE + STRIP)
    here = me * size
    extra = jnp.where(in_right, here + size + place, jnp.where(in_left, here - size + place, place - BASE))
    valid = (in_right & has_right) | (in_left & has_left) | in_strip
    extra = jnp.where(valid, extra, 0)
    keep = jnp.where(valid, 1.0, 0.0).astype(F32)
    flip = jnp.where(second, -keep, keep)
    positions = jnp.concatenate([here + row_lane, here + ((row_lane + 64) & (size - 1)), extra[0:1, :]], axis=1)
    radial = inner_radius + (positions + 1).astype(F32) * spacing
    inverse = 1.0 / (radial * radial)

    @pl.when(has_right)
    def _():
        left_copy_in = halo_copy(left_half, right_in, 0, jnp.minimum(me + 1, count - 1))
        left_copy_in.wait_recv()

    @pl.when(jnp.logical_not(has_right))
    def _():
        right_in[...] = jnp.zeros_like(right_in)

    @pl.when(has_left)
    def _():
        right_copy_in = halo_copy(right_half, left_in, 1, jnp.maximum(me - 1, 0))
        right_copy_in.wait_recv()

    @pl.when(jnp.logical_not(has_left))
    def _():
        left_in[...] = jnp.zeros_like(left_in)

    def stretch(index, _):
        near_rows = pl.ds(pl.multiple_of(index * ROWS, ROWS), ROWS)
        far_rows = pl.ds(pl.multiple_of(message + index * ROWS, ROWS), ROWS)
        right, left = right_in[near_rows, :], left_in[near_rows, :]
        from_right[near_rows, :] = right
        from_right[far_rows, :] = pltpu.roll(right, size - HALO, 1)
        from_left[near_rows, :] = left
        from_left[far_rows, :] = pltpu.roll(left, HALO, 1)
        return 0

    lax.fori_loop(0, message // ROWS, stretch, 0)

    def unpack(cut, pair):
        right, left, inner = from_right[cut, :], from_left[cut, :], strip[cut, :]
        if pair == 1:
            right, left = pltpu.roll(right, 96, 1), pltpu.roll(left, 32, 1)
        inner = pltpu.roll(inner, BASE if pair == 0 else BASE + 96, 1)
        found = jnp.where(in_right, right, jnp.where(in_left, left, inner))
        return jnp.where(valid, found, 0.0)

    def shift(value, amount):
        return pltpu.roll(value, amount % size, 1)

    def wide(pair, tile):
        first = 4 * size + pair * size if tile == 2 else 2 * pair * size + tile * size
        return slice(first, first + size)

    near = ((lane & 63) >= BASE) & ((lane & 63) < BASE + 4)

    def store_tile(pair, tile, start, value):
        cols = wide(pair, tile)
        high, rest = halves(value)
        if tile == 2:
            again = pltpu.roll(jnp.where(near, high.astype(F32), 0.0), AGAIN, 1)
            high = (high.astype(F32) + again).astype(BF16)
        rhs[pl.ds(start, ROWS), cols] = high
        rhs[pl.ds(channels + start, ROWS), cols] = rest
        rhs[pl.ds(2 * channels + start, ROWS), cols] = high

    def store_split(pair, start, tiles):
        for tile, value in enumerate(tiles):
            store_tile(pair, tile, start, value)

    unit = 0.5 / (spacing * spacing) / 12.0
    prof_extra = unpack(slice(channels, channels + extra_rows), 0)
    prof_all = jnp.concatenate([padded_prof, turned_prof, prof_extra], axis=1)
    row = lax.broadcasted_iota(jnp.int32, (size, 1), 0)
    spot = row & 63
    again = (spot >= BASE + AGAIN) & (spot < BASE + AGAIN + 4)
    point = spot - BASE
    def weights(values):
        found = jnp.zeros((size, 1), F32)
        for index, value in enumerate(values):
            found = jnp.where(point == index, value / unit, found)
        return found

    value_weight = weights((4.0, -6.0, 4.0, -1.0))
    slope_weight = weights((-13.0 / 3.0, 9.5, -7.0, 11.0 / 6.0))
    owner = jnp.concatenate([jnp.zeros((1, size), jnp.int32), jnp.ones((1, size), jnp.int32), jnp.where(second, 1, 0)[0:1, :]], axis=1)
    full = value_weight * prof_all[0:1, :] + slope_weight * prof_all[1:2, :]
    full = jnp.where((row >> 6) == owner, full, 0.0)

    def chain(index):
        tile, at = index >> 7, index & (size - 1)
        half = (at + 64) & (size - 1)
        other = (at >= 48) & (at < 112)
        spot = jnp.where(other, half, at)
        place = jnp.where(spot < HALO, spot + size, jnp.where(spot >= size - HALO, spot - size, 1000 + spot))
        inside = (spot < BASE + STRIP) | (spot >= size - HALO)
        inside = inside & ((spot < HALO) | (spot >= BASE))
        place = jnp.where(inside, place + jnp.where(other, 4000, 0), 10000 + 10 * at)
        return jnp.where(tile == 0, at, jnp.where(tile == 1, 4000 + half, place))

    across = chain(lax.broadcasted_iota(jnp.int32, (1, 3 * size), 1))
    for tile in range(3):
        down = chain(row + tile * size)
        apart = jnp.abs(down - across)
        band = jnp.where(apart == 2, 1.0, jnp.where(apart == 1, -16.0, 0.0))
        if tile == 2:
            band = band + full
        high = band.astype(BF16)
        if tile == 2:
            low_part = pltpu.roll(band - high.astype(F32), AGAIN, 0)
            high = jnp.where(again, low_part, high.astype(F32)).astype(BF16)
        for copy in range(2):
            first = (3 * copy + tile) * size
            surface[first : first + size, :] = high

    rhs[3 * channels :, :] = jnp.zeros((rhs.shape[0] - 3 * channels, 6 * size), BF16)
    diagonal = 1.25 / (spacing * spacing) / unit

    def begin(start, carry):
        rows = pl.ds(start, ROWS)
        for tile in range(3):
            cols = slice(tile * size, (tile + 1) * size)
            level = columns[0, rows, :] + columns[1, rows, :] * inverse[:, cols]
            pot[rows, cols] = level / unit + diagonal
        for pair in range(2):
            tiles = [term[pair, rows, 0:size], term[pair, rows, size : 2 * size], unpack(rows, pair)]
            term[pair, rows, 2 * size :] = tiles[2]
            store_split(pair, start, tiles)
            total[0, pair, rows, :] = jnp.concatenate(tiles, axis=1)
            total[1, pair, rows, :] = jnp.zeros((ROWS, 3 * size), F32)
        return carry

    over_rows(begin)

    def grad_copy(other, slot):
        return pltpu.make_async_remote_copy(
            src_ref=partial, dst_ref=gathered.at[slot], send_sem=grad_send.at[other],
            recv_sem=grad_recv.at[slot], device_id={"radius": other}, device_id_type=MESH,
        )

    def one_step(step, _):
        strength = pulse[step]
        driven = (strength / unit) * radial

        def one_term(index, _):
            power = index + 1
            scale = unit * time_step / power.astype(F32)
            odd = lax.rem(power, 2)
            signed = jnp.where(odd == 1, -scale, scale)

            stacked = []
            for pair in range(2):
                tiles = [rhs[part : part + channels, wide(pair, tile)] for part in (0, channels) for tile in range(3)]
                stacked.append(jnp.concatenate(tiles, axis=1))
            bound[...] = jnp.dot(jnp.concatenate(stacked, axis=0), surface[...], preferred_element_type=F32)

            def mix(block):
                cols = slice(block * 2 * size, (block + 1) * 2 * size)
                mixed[:, cols] = jnp.dot(lhs[0:channels, :], rhs[:, cols], preferred_element_type=F32)

            mix(0)

            @pl.when(index == 0)
            def _():
                def meet(start, found):
                    rows = pl.ds(start, ROWS)
                    turned = shift(mixed[rows, size : 2 * size], 64) * term[1, rows, 0:size]
                    straight = shift(term[1, rows, size : 2 * size], 64) * mixed[rows, 0:size]
                    both = turned - straight
                    return found + both[0:8] + both[8:16]

                partial[step] = over_rows(meet, jnp.zeros((8, size), F32)) * radial[:, 0:size]

                @pl.when(step == STEPS - 1)
                def _():
                    def send(d, _):
                        grad_copy(lax.rem(me + d, count), me).start()
                        return 0

                    lax.fori_loop(1, count, send, 0)

            def advance(pair, tile):
                cols = slice(tile * size, (tile + 1) * size)
                factor = (signed, -signed, signed * flip)[tile]
                spread_driven = jnp.broadcast_to(driven[:, cols], (ROWS, size))
                for start in range(0, channels, ROWS):
                    rows = slice(start, start + ROWS)
                    value = bound[pair * channels + start : pair * channels + start + ROWS, cols]
                    value = value + pot[rows, cols] * term[pair, rows, cols]
                    value = value + spread_driven * mixed[rows, wide(pair, tile)]
                    value = factor * value
                    term[pair, rows, cols] = value
                    total[odd, pair, rows, cols] += value
                    store_tile(pair, tile, start, value)

            mix(1)
            advance(0, 0)
            advance(0, 1)
            mix(2)
            advance(1, 0)
            advance(1, 1)
            advance(0, 2)
            advance(1, 2)
            return 0

        lax.fori_loop(0, ORDER, one_term, 0)

        def close(start, carry):
            rows = pl.ds(start, ROWS)
            for pair in range(2):
                tiles = []
                for tile in range(3):
                    cols = slice(tile * size, (tile + 1) * size)
                    source = (1, 0, 2)[tile]
                    turned = shift(total[1, pair, rows, source * size : (source + 1) * size], 64)
                    tiles.append(total[0, pair, rows, cols] + turned)
                for tile in range(3):
                    cols = slice(tile * size, (tile + 1) * size)
                    term[pair, rows, cols] = tiles[tile]
                    total[0, pair, rows, cols] = tiles[tile]
                    total[1, pair, rows, cols] = jnp.zeros((ROWS, size), F32)
                store_split(pair, start, tiles)
            return carry

        over_rows(close)
        return 0

    lax.fori_loop(0, STEPS, one_step, 0)

    def finish_rows(start, carry):
        rows = pl.ds(start, ROWS)
        for pair in range(2):
            out[2 * pair, rows, :] = term[pair, rows, 0:size]
            out[2 * pair + 1, rows, :] = shift(term[pair, rows, size : 2 * size], 64)
        return carry

    over_rows(finish_rows)

    gathered[me] = partial[...]

    def collect(d, _):
        other = lax.rem(me + d, count)
        copy = grad_copy(other, other)
        copy.wait_recv()
        return 0

    lax.fori_loop(1, count, collect, 0)
    normalizer = math.sqrt(channels * count * size) * (inner_radius + count * size * spacing)
    for step in range(STEPS):
        found = jnp.zeros((8, size), F32)
        for index in range(count):
            found = found + gathered[index, step]
        grad[step] = jnp.sum(found) / normalizer

    def finish(d, _):
        grad_copy(lax.rem(me + d, count), me).wait_send()
        return 0

    lax.fori_loop(1, count, finish, 0)

    @pl.when(has_left)
    def _():
        left_copy.wait_send()

    @pl.when(has_right)
    def _():
        right_copy.wait_send()

    for which in range(len(TREE)):
        @pl.when(children[which][1])
        def _():
            for part in range(CHUNKS):
                strip_copy(part, which).wait_send()


def per_device(count, states, dipole, pattern, angular, thresholds, surface_profile, pulse_field):
    channels = states.shape[1]
    size = states.shape[2]
    padded = -(-channels // BLOCK) * BLOCK
    depth = -(-3 * channels // 256) * 256
    angular, thresholds = angular[None, :], thresholds[None, :]
    vmem = pl.BlockSpec(memory_space=pltpu.VMEM)
    smem = pl.BlockSpec(memory_space=pltpu.SMEM)
    message = pltpu.VMEM((channels + 16, size), F32)
    half = pltpu.VMEM(((channels + 16) // 2, size), F32)
    wide = (2, channels, 3 * size)
    return pl.pallas_call(
        functools.partial(kernel, count, channels),
        out_shape=(
            jax.ShapeDtypeStruct(states.shape, F32),
            jax.ShapeDtypeStruct(pulse_field.shape, F32),
        ),
        in_specs=[pl.BlockSpec(memory_space=pltpu.HBM)] * 6 + [smem],
        out_specs=(vmem, smem),
        scratch_shapes=[
            message, message, message, message, message, half, half, half, half,
            pltpu.VMEM(wide, F32),
            pltpu.VMEM((2,) + wide, F32),
            pltpu.VMEM((depth, 6 * size), BF16),
            pltpu.VMEM((channels, 6 * size), F32),
            pltpu.VMEM((2 * channels, 3 * size), F32),
            pltpu.VMEM((6 * size, 3 * size), BF16),
            pltpu.VMEM((channels, 3 * size), F32),
            pltpu.VMEM((STEPS, 8, size), F32),
            pltpu.VMEM((count, STEPS, 8, size), F32),
            pltpu.VMEM((padded, depth), BF16),
            pltpu.VMEM((padded, padded), F32),
            pltpu.VMEM((BLOCK, BLOCK), F32),
            pltpu.VMEM((2, padded, BLOCK), F32),
            pltpu.VMEM(states.shape, F32),
            pltpu.VMEM(dipole.shape, F32),
            pltpu.VMEM(pattern.shape, jnp.int32),
            pltpu.VMEM(angular.shape, jnp.int32),
            pltpu.VMEM(thresholds.shape, F32),
            pltpu.VMEM((8, padded), F32),
            pltpu.VMEM(surface_profile.shape, F32),
            pltpu.SemaphoreType.DMA((6,)),
            pltpu.SemaphoreType.DMA((2,)),
            pltpu.SemaphoreType.DMA((2,)),
            pltpu.SemaphoreType.DMA((len(TREE), CHUNKS)),
            pltpu.SemaphoreType.DMA((CHUNKS,)),
            pltpu.SemaphoreType.DMA((count,)),
            pltpu.SemaphoreType.DMA((count,)),
        ],
        compiler_params=pltpu.CompilerParams(
            collective_id=0, has_side_effects=True, vmem_limit_bytes=63 * 1024 * 1024
        ),
        cost_estimate=pl.CostEstimate(flops=8000000000, bytes_accessed=4000000, transcendentals=0),
    )(states, dipole, pattern, angular, thresholds, surface_profile, pulse_field)


def solution(mesh):
    return jax.shard_map(
        functools.partial(per_device, mesh.shape["radius"]),
        mesh=mesh,
        in_specs=(P("groups", None, "radius"), P(), P(), P(), P(), P(None, "radius"), P("groups")),
        out_specs=(P("groups", None, "radius"), P("groups")),
        check_vma=False,
    )
```

```python
import functools
import math

import jax
import jax.numpy as jnp
from jax import lax
from jax.experimental import pallas as pl
from jax.experimental.pallas import tpu as pltpu
from jax.sharding import PartitionSpec as P

STEPS = 2
ORDER = 4
inner_radius = 20.0
spacing = 0.08
time_step = 0.005

HALO = 2 * ORDER * STEPS
STRIP = HALO + 2
BASE = 20
ROWS = 16
CHUNKS = 13
BLOCK = 128
AGAIN = 18
GROUP = 5
TREE = (4, 2, 1)
MESH = pl.DeviceIdType.MESH
F32 = jnp.float32
BF16 = jnp.bfloat16


def halves(value):
    high = value.astype(BF16)
    return high, (value - high.astype(F32)).astype(BF16)


def build_coupling(channels, dipole, pattern, chan, square, joined, columns, lhs):
    blocks = pattern.shape[0]
    parts = square.shape[0] // BLOCK
    owned = channels // blocks
    square[...] = jnp.zeros_like(square)
    square[0:channels, 0:channels] = dipole[...]
    joined[...] = jnp.zeros_like(joined)
    joined[0:blocks, 0:blocks] = pattern[...].astype(F32)
    either = jnp.maximum(joined[...], joined[...].T).astype(BF16)
    lane = lax.broadcasted_iota(jnp.int32, (BLOCK, BLOCK), 1)
    row = lax.broadcasted_iota(jnp.int32, (BLOCK, BLOCK), 0)

    def pick(place, block):
        first = block * owned
        return jnp.where((place >= first) & (place < first + owned), 1.0, 0.0).astype(BF16)

    def spread(which, part):
        return jnp.broadcast_to(chan[which : which + 1, part * BLOCK : (part + 1) * BLOCK], (BLOCK, BLOCK))

    across = [spread(0, part) for part in range(parts)]
    picks = pick(
        lax.broadcasted_iota(jnp.int32, (BLOCK, parts * BLOCK), 1),
        lax.broadcasted_iota(jnp.int32, (BLOCK, parts * BLOCK), 0),
    )
    for i in range(parts):
        down = across[i].T
        rows = slice(i * BLOCK, (i + 1) * BLOCK)
        columns[0, rows, :] = spread(1, i).T
        columns[1, rows, :] = 0.5 * (down * (down + 1.0))
        held = jnp.dot(pick(row + i * BLOCK, lane), either, preferred_element_type=F32).astype(BF16)
        masks = jnp.dot(held, picks, preferred_element_type=F32)
        found = {}
        for j in range(parts):
            cols = slice(j * BLOCK, (j + 1) * BLOCK)
            allowed = (masks[:, cols] > 0.5) & (jnp.abs(down - across[j]) == 1.0)
            mean = 0.5 * (square[rows, cols] + square[cols, rows].T)
            coupling = jnp.where(allowed, mean, 0.0)
            high = coupling.astype(BF16).astype(F32)
            rest = coupling - high
            for copy, value in enumerate((high, high, rest)):
                place = copy * channels + j * BLOCK
                tile, off = place // BLOCK, place % BLOCK
                moved = pltpu.roll(value, off, 1) if off else value
                for tile, kept in ((tile, lane >= off), (tile + 1, lane < off)):
                    if tile in found:
                        found[tile] = found[tile] + jnp.where(kept, moved, 0.0)
                    elif tile < lhs.shape[1] // BLOCK:
                        found[tile] = jnp.where(kept, moved, 0.0)
        for tile, value in found.items():
            lhs[rows, tile * BLOCK : (tile + 1) * BLOCK] = value.astype(BF16)


def kernel(
    count, channels, states_in, dipole_in, pattern_in, angular_in, thresholds_in, prof_in, pulse, out, grad,
    to_left, to_right, from_left, from_right, strip, left_half, right_half, left_in, right_in,
    term, total, rhs, mixed, bound, surface, pot, partial, gathered,
    lhs, square, joined, columns, states, dipole, pattern, angular, thresholds, chan, prof, load,
    halo_send, halo_recv, strip_send, strip_recv, grad_send, grad_recv,
):
    me = lax.axis_index("radius")
    size = 128
    has_left, has_right = me > 0, me < count - 1
    lane = lax.broadcasted_iota(jnp.int32, (ROWS, size), 1)
    row_lane = lane[0:1, :]
    extra_rows = 16
    loads = [
        pltpu.make_async_copy(source, target, load.at[which])
        for which, (source, target) in enumerate(
            ((states_in, states), (prof_in, prof), (dipole_in, dipole), (pattern_in, pattern), (angular_in, angular), (thresholds_in, thresholds))
        )
    ]
    for copy in loads:
        copy.start()

    def over_rows(body, carry=0):
        def several(index, carry):
            for part in range(GROUP):
                carry = body(pl.multiple_of((index * GROUP + part) * ROWS, ROWS), carry)
            return carry

        return lax.fori_loop(0, channels // ROWS // GROUP, several, carry)

    barrier = pltpu.get_barrier_semaphore()

    def greet(d, _):
        other = lax.rem(me + d, count)
        pl.semaphore_signal(barrier, inc=1, device_id={"radius": other}, device_id_type=MESH)
        return 0

    lax.fori_loop(1, count, greet, 0)

    loads[0].wait()
    loads[1].wait()
    low = lane < 64
    low_quarter = (lane & 63) < 32
    padded_prof = jnp.concatenate([prof[...], jnp.zeros((extra_rows - 2, size), F32)], axis=0)
    turned_prof = pltpu.roll(padded_prof, 64, 1)

    def pack(rows, parts):
        a, b, c, d = parts
        left = jnp.where(low_quarter, jnp.where(low, a, b), pltpu.roll(jnp.where(low, c, d), 32, 1))
        right = jnp.where(low_quarter, pltpu.roll(jnp.where(low, d, c), 96, 1), jnp.where(low, b, a))
        to_left[rows, :] = left
        to_right[rows, :] = right

    def pack_rows(start, carry):
        rows = pl.ds(start, ROWS)
        a, c = states[0, rows, :], states[2, rows, :]
        b, d = pltpu.roll(states[1, rows, :], 64, 1), pltpu.roll(states[3, rows, :], 64, 1)
        pack(rows, (a, b, c, d))
        for pair, (first, other) in enumerate(((a, b), (c, d))):
            term[pair, rows, 0:size] = first
            term[pair, rows, size : 2 * size] = other
        return carry

    over_rows(pack_rows)
    pack(slice(channels, channels + extra_rows), (padded_prof, turned_prof, padded_prof, turned_prof))

    @pl.when(me == 0)
    def _():
        strip[...] = to_left[...]

    message = (channels + extra_rows) // 2
    first_half = (lane & 31) < HALO

    def squeeze(index, _):
        near_rows = pl.ds(pl.multiple_of(index * ROWS, ROWS), ROWS)
        far_rows = pl.ds(pl.multiple_of(message + index * ROWS, ROWS), ROWS)
        left_half[near_rows, :] = jnp.where(first_half, to_left[near_rows, :], pltpu.roll(to_left[far_rows, :], HALO, 1))
        right_half[near_rows, :] = jnp.where(
            first_half, pltpu.roll(to_right[far_rows, :], size - HALO, 1), to_right[near_rows, :]
        )
        return 0

    lax.fori_loop(0, message // ROWS, squeeze, 0)

    pl.semaphore_wait(barrier, count - 1)

    def halo_copy(source, target, which, other):
        return pltpu.make_async_remote_copy(
            src_ref=source, dst_ref=target, send_sem=halo_send.at[which],
            recv_sem=halo_recv.at[which], device_id={"radius": other}, device_id_type=MESH,
        )

    left_copy = halo_copy(left_half, right_in, 0, jnp.maximum(me - 1, 0))
    right_copy = halo_copy(right_half, left_in, 1, jnp.minimum(me + 1, count - 1))

    chunk = (channels + extra_rows) // CHUNKS
    children = []
    for step in TREE:
        child = me + step
        mine = (lax.rem(me, 2 * step) == 0) if step < TREE[0] else (lax.rem(me, step) == 0)
        children.append((child, mine & (child < count)))

    def strip_copy(part, which):
        rows = pl.ds(part * chunk, chunk)
        return pltpu.make_async_remote_copy(
            src_ref=strip.at[rows, :], dst_ref=strip.at[rows, :],
            send_sem=strip_send.at[which, part], recv_sem=strip_recv.at[part],
            device_id={"radius": jnp.minimum(children[which][0], count - 1)}, device_id_type=MESH,
        )

    def send_on(part):
        for which in range(len(TREE)):
            @pl.when(children[which][1])
            def _():
                strip_copy(part, which).start()

    @pl.when(me == 0)
    def _():
        for part in range(CHUNKS):
            send_on(part)

    @pl.when(has_left)
    def _():
        left_copy.start()

    @pl.when(has_right)
    def _():
        right_copy.start()

    for copy in loads[2:]:
        copy.wait()
    chan[...] = jnp.zeros_like(chan)
    chan[0:1, 0:channels] = angular[...].astype(F32)
    chan[1:2, 0:channels] = thresholds[...]
    second = (lane >= 48) & (lane < 112)
    place = jnp.where(second, ((lane + 64) & (size - 1)), lane)
    in_right, in_left = place < HALO, place >= size - HALO
    in_strip = (place >= BASE) & (place < BASE + STRIP)
    here = me * size
    extra = jnp.where(in_right, here + size + place, jnp.where(in_left, here - size + place, place - BASE))
    valid = (in_right & has_right) | (in_left & has_left) | in_strip
    extra = jnp.where(valid, extra, 0)
    keep = jnp.where(valid, 1.0, 0.0).astype(F32)
    flip = jnp.where(second, -keep, keep)
    positions = jnp.concatenate([here + row_lane, here + ((row_lane + 64) & (size - 1)), extra[0:1, :]], axis=1)
    radial = inner_radius + (positions + 1).astype(F32) * spacing
    inverse = 1.0 / (radial * radial)

    unit = 0.5 / (spacing * spacing) / 12.0
    row = lax.broadcasted_iota(jnp.int32, (size, 1), 0)
    def wide(pair, tile):
        first = 4 * size + pair * size if tile == 2 else 2 * pair * size + tile * size
        return slice(first, first + size)

    near = ((lane & 63) >= BASE) & ((lane & 63) < BASE + 4)

    def store_tile(pair, tile, start, value):
        cols = wide(pair, tile)
        high, rest = halves(value)
        if tile == 2:
            again = pltpu.roll(jnp.where(near, high.astype(F32), 0.0), AGAIN, 1)
            high = (high.astype(F32) + again).astype(BF16)
        rhs[pl.ds(start, ROWS), cols] = high
        rhs[pl.ds(channels + start, ROWS), cols] = rest
        rhs[pl.ds(2 * channels + start, ROWS), cols] = high

    def store_split(pair, start, tiles):
        for tile, value in enumerate(tiles):
            store_tile(pair, tile, start, value)

    def chain(index):
        tile, at = index >> 7, index & (size - 1)
        half = (at + 64) & (size - 1)
        other = (at >= 48) & (at < 112)
        spot = jnp.where(other, half, at)
        place = jnp.where(spot < HALO, spot + size, jnp.where(spot >= size - HALO, spot - size, 1000 + spot))
        inside = (spot < BASE + STRIP) | (spot >= size - HALO)
        inside = inside & ((spot < HALO) | (spot >= BASE))
        place = jnp.where(inside, place + jnp.where(other, 4000, 0), 10000 + 10 * at)
        return jnp.where(tile == 0, at, jnp.where(tile == 1, 4000 + half, place))

    across = chain(lax.broadcasted_iota(jnp.int32, (1, 3 * size), 1))
    def band_rows(tile):
        apart = jnp.abs(chain(row + tile * size) - across)
        return jnp.where(apart == 2, 1.0, jnp.where(apart == 1, -16.0, 0.0))

    def store_band(tile, value):
        for copy in range(2):
            first = (3 * copy + tile) * size
            surface[first : first + size, :] = value

    diagonal = 1.25 / (spacing * spacing) / unit

    def begin(start, carry):
        rows = pl.ds(start, ROWS)
        for tile in range(3):
            cols = slice(tile * size, (tile + 1) * size)
            level = columns[0, rows, :] + columns[1, rows, :] * inverse[:, cols]
            pot[rows, cols] = level / unit + diagonal
        for pair in range(2):
            for tile in range(2):
                cols = slice(tile * size, (tile + 1) * size)
                value = term[pair, rows, cols]
                store_tile(pair, tile, start, value)
                total[0, pair, rows, cols] = value
            total[1, pair, rows, :] = jnp.zeros((ROWS, 3 * size), F32)
        return carry

    pass_first = (lax.rem(me, TREE[0]) == 0) & (me > 0) & (me <= count // 2)
    build_phase = jnp.where(pass_first, 1, 0)

    def phase(which, _):
        @pl.when(which == build_phase)
        def _():
            build_coupling(channels, dipole, pattern, chan, square, joined, columns, lhs)
            for tile in range(2):
                store_band(tile, band_rows(tile).astype(BF16))
            rhs[3 * channels :, :] = jnp.zeros((rhs.shape[0] - 3 * channels, 6 * size), BF16)
            over_rows(begin)

        @pl.when((which != build_phase) & (me > 0))
        def _():
            for part in range(CHUNKS):
                strip_copy(part, 0).wait_recv()
                send_on(part)

        return 0

    lax.fori_loop(0, 2, phase, 0)

    @pl.when(has_right)
    def _():
        left_copy_in = halo_copy(left_half, right_in, 0, jnp.minimum(me + 1, count - 1))
        left_copy_in.wait_recv()

    @pl.when(jnp.logical_not(has_right))
    def _():
        right_in[...] = jnp.zeros_like(right_in)

    @pl.when(has_left)
    def _():
        right_copy_in = halo_copy(right_half, left_in, 1, jnp.maximum(me - 1, 0))
        right_copy_in.wait_recv()

    @pl.when(jnp.logical_not(has_left))
    def _():
        left_in[...] = jnp.zeros_like(left_in)

    def stretch(index, _):
        near_rows = pl.ds(pl.multiple_of(index * ROWS, ROWS), ROWS)
        far_rows = pl.ds(pl.multiple_of(message + index * ROWS, ROWS), ROWS)
        right, left = right_in[near_rows, :], left_in[near_rows, :]
        from_right[near_rows, :] = right
        from_right[far_rows, :] = pltpu.roll(right, size - HALO, 1)
        from_left[near_rows, :] = left
        from_left[far_rows, :] = pltpu.roll(left, HALO, 1)
        return 0

    lax.fori_loop(0, message // ROWS, stretch, 0)

    def unpack(cut, pair):
        right, left, inner = from_right[cut, :], from_left[cut, :], strip[cut, :]
        if pair == 1:
            right, left = pltpu.roll(right, 96, 1), pltpu.roll(left, 32, 1)
        inner = pltpu.roll(inner, BASE if pair == 0 else BASE + 96, 1)
        found = jnp.where(in_right, right, jnp.where(in_left, left, inner))
        return jnp.where(valid, found, 0.0)

    def shift(value, amount):
        return pltpu.roll(value, amount % size, 1)

    prof_extra = unpack(slice(channels, channels + extra_rows), 0)
    prof_all = jnp.concatenate([padded_prof, turned_prof, prof_extra], axis=1)
    spot = row & 63
    again = (spot >= BASE + AGAIN) & (spot < BASE + AGAIN + 4)
    point = spot - BASE
    def weights(values):
        found = jnp.zeros((size, 1), F32)
        for index, value in enumerate(values):
            found = jnp.where(point == index, value / unit, found)
        return found

    value_weight = weights((4.0, -6.0, 4.0, -1.0))
    slope_weight = weights((-13.0 / 3.0, 9.5, -7.0, 11.0 / 6.0))
    owner = jnp.concatenate([jnp.zeros((1, size), jnp.int32), jnp.ones((1, size), jnp.int32), jnp.where(second, 1, 0)[0:1, :]], axis=1)
    full = value_weight * prof_all[0:1, :] + slope_weight * prof_all[1:2, :]
    full = jnp.where((row >> 6) == owner, full, 0.0)

    band = band_rows(2) + full
    high = band.astype(BF16)
    low_part = pltpu.roll(band - high.astype(F32), AGAIN, 0)
    store_band(2, jnp.where(again, low_part, high.astype(F32)).astype(BF16))

    def begin_extra(start, carry):
        rows = pl.ds(start, ROWS)
        for pair in range(2):
            value = unpack(rows, pair)
            term[pair, rows, 2 * size :] = value
            total[0, pair, rows, 2 * size :] = value
            store_tile(pair, 2, start, value)
        return carry

    over_rows(begin_extra)

    def grad_copy(other, slot):
        return pltpu.make_async_remote_copy(
            src_ref=partial, dst_ref=gathered.at[slot], send_sem=grad_send.at[other],
            recv_sem=grad_recv.at[slot], device_id={"radius": other}, device_id_type=MESH,
        )

    def one_step(step, _):
        strength = pulse[step]
        driven = (strength / unit) * radial

        def one_term(index, _):
            power = index + 1
            scale = unit * time_step / power.astype(F32)
            odd = lax.rem(power, 2)
            signed = jnp.where(odd == 1, -scale, scale)

            stacked = []
            for pair in range(2):
                tiles = [rhs[part : part + channels, wide(pair, tile)] for part in (0, channels) for tile in range(3)]
                stacked.append(jnp.concatenate(tiles, axis=1))
            bound[...] = jnp.dot(jnp.concatenate(stacked, axis=0), surface[...], preferred_element_type=F32)

            def mix(block):
                cols = slice(block * 2 * size, (block + 1) * 2 * size)
                mixed[:, cols] = jnp.dot(lhs[0:channels, :], rhs[:, cols], preferred_element_type=F32)

            mix(0)

            @pl.when(index == 0)
            def _():
                def meet(start, found):
                    rows = pl.ds(start, ROWS)
                    turned = shift(mixed[rows, size : 2 * size], 64) * term[1, rows, 0:size]
                    straight = shift(term[1, rows, size : 2 * size], 64) * mixed[rows, 0:size]
                    both = turned - straight
                    return found + both[0:8] + both[8:16]

                partial[step] = over_rows(meet, jnp.zeros((8, size), F32)) * radial[:, 0:size]

                @pl.when(step == STEPS - 1)
                def _():
                    def send(d, _):
                        grad_copy(lax.rem(me + d, count), me).start()
                        return 0

                    lax.fori_loop(1, count, send, 0)

            def advance(pair, tile):
                cols = slice(tile * size, (tile + 1) * size)
                factor = (signed, -signed, signed * flip)[tile]
                spread_driven = jnp.broadcast_to(driven[:, cols], (ROWS, size))
                for start in range(0, channels, ROWS):
                    rows = slice(start, start + ROWS)
                    value = bound[pair * channels + start : pair * channels + start + ROWS, cols]
                    value = value + pot[rows, cols] * term[pair, rows, cols]
                    value = value + spread_driven * mixed[rows, wide(pair, tile)]
                    value = factor * value
                    term[pair, rows, cols] = value
                    total[odd, pair, rows, cols] += value
                    store_tile(pair, tile, start, value)

            mix(1)
            advance(0, 0)
            advance(0, 1)
            mix(2)
            advance(1, 0)
            advance(1, 1)
            advance(0, 2)
            advance(1, 2)
            return 0

        lax.fori_loop(0, ORDER, one_term, 0)

        def close(start, carry):
            rows = pl.ds(start, ROWS)
            for pair in range(2):
                tiles = []
                for tile in range(3):
                    cols = slice(tile * size, (tile + 1) * size)
                    source = (1, 0, 2)[tile]
                    turned = shift(total[1, pair, rows, source * size : (source + 1) * size], 64)
                    tiles.append(total[0, pair, rows, cols] + turned)
                for tile in range(3):
                    cols = slice(tile * size, (tile + 1) * size)
                    term[pair, rows, cols] = tiles[tile]
                    total[0, pair, rows, cols] = tiles[tile]
                    total[1, pair, rows, cols] = jnp.zeros((ROWS, size), F32)
                store_split(pair, start, tiles)
            return carry

        over_rows(close)
        return 0

    lax.fori_loop(0, STEPS, one_step, 0)

    def finish_rows(start, carry):
        rows = pl.ds(start, ROWS)
        for pair in range(2):
            out[2 * pair, rows, :] = term[pair, rows, 0:size]
            out[2 * pair + 1, rows, :] = shift(term[pair, rows, size : 2 * size], 64)
        return carry

    over_rows(finish_rows)

    gathered[me] = partial[...]

    def collect(d, _):
        other = lax.rem(me + d, count)
        copy = grad_copy(other, other)
        copy.wait_recv()
        return 0

    lax.fori_loop(1, count, collect, 0)
    normalizer = math.sqrt(channels * count * size) * (inner_radius + count * size * spacing)
    for step in range(STEPS):
        found = jnp.zeros((8, size), F32)
        for index in range(count):
            found = found + gathered[index, step]
        grad[step] = jnp.sum(found) / normalizer

    def finish(d, _):
        grad_copy(lax.rem(me + d, count), me).wait_send()
        return 0

    lax.fori_loop(1, count, finish, 0)

    @pl.when(has_left)
    def _():
        left_copy.wait_send()

    @pl.when(has_right)
    def _():
        right_copy.wait_send()

    for which in range(len(TREE)):
        @pl.when(children[which][1])
        def _():
            for part in range(CHUNKS):
                strip_copy(part, which).wait_send()


def per_device(count, states, dipole, pattern, angular, thresholds, surface_profile, pulse_field):
    channels = states.shape[1]
    size = states.shape[2]
    padded = -(-channels // BLOCK) * BLOCK
    depth = -(-3 * channels // 256) * 256
    angular, thresholds = angular[None, :], thresholds[None, :]
    vmem = pl.BlockSpec(memory_space=pltpu.VMEM)
    smem = pl.BlockSpec(memory_space=pltpu.SMEM)
    message = pltpu.VMEM((channels + 16, size), F32)
    half = pltpu.VMEM(((channels + 16) // 2, size), F32)
    wide = (2, channels, 3 * size)
    return pl.pallas_call(
        functools.partial(kernel, count, channels),
        out_shape=(
            jax.ShapeDtypeStruct(states.shape, F32),
            jax.ShapeDtypeStruct(pulse_field.shape, F32),
        ),
        in_specs=[pl.BlockSpec(memory_space=pltpu.HBM)] * 6 + [smem],
        out_specs=(vmem, smem),
        scratch_shapes=[
            message, message, message, message, message, half, half, half, half,
            pltpu.VMEM(wide, F32),
            pltpu.VMEM((2,) + wide, F32),
            pltpu.VMEM((depth, 6 * size), BF16),
            pltpu.VMEM((channels, 6 * size), F32),
            pltpu.VMEM((2 * channels, 3 * size), F32),
            pltpu.VMEM((6 * size, 3 * size), BF16),
            pltpu.VMEM((channels, 3 * size), F32),
            pltpu.VMEM((STEPS, 8, size), F32),
            pltpu.VMEM((count, STEPS, 8, size), F32),
            pltpu.VMEM((padded, depth), BF16),
            pltpu.VMEM((padded, padded), F32),
            pltpu.VMEM((BLOCK, BLOCK), F32),
            pltpu.VMEM((2, padded, BLOCK), F32),
            pltpu.VMEM(states.shape, F32),
            pltpu.VMEM(dipole.shape, F32),
            pltpu.VMEM(pattern.shape, jnp.int32),
            pltpu.VMEM(angular.shape, jnp.int32),
            pltpu.VMEM(thresholds.shape, F32),
            pltpu.VMEM((8, padded), F32),
            pltpu.VMEM(surface_profile.shape, F32),
            pltpu.SemaphoreType.DMA((6,)),
            pltpu.SemaphoreType.DMA((2,)),
            pltpu.SemaphoreType.DMA((2,)),
            pltpu.SemaphoreType.DMA((len(TREE), CHUNKS)),
            pltpu.SemaphoreType.DMA((CHUNKS,)),
            pltpu.SemaphoreType.DMA((count,)),
            pltpu.SemaphoreType.DMA((count,)),
        ],
        compiler_params=pltpu.CompilerParams(
            collective_id=0, has_side_effects=True, vmem_limit_bytes=63 * 1024 * 1024
        ),
        cost_estimate=pl.CostEstimate(flops=8000000000, bytes_accessed=4000000, transcendentals=0),
    )(states, dipole, pattern, angular, thresholds, surface_profile, pulse_field)


def solution(mesh):
    return jax.shard_map(
        functools.partial(per_device, mesh.shape["radius"]),
        mesh=mesh,
        in_specs=(P("groups", None, "radius"), P(), P(), P(), P(), P(None, "radius"), P("groups")),
        out_specs=(P("groups", None, "radius"), P("groups")),
        check_vma=False,
    )
```

```python
import functools
import math

import jax
import jax.numpy as jnp
from jax import lax
from jax.experimental import pallas as pl
from jax.experimental.pallas import tpu as pltpu
from jax.sharding import PartitionSpec as P

STEPS = 2
ORDER = 4
inner_radius = 20.0
spacing = 0.08
time_step = 0.005

HALO = 2 * ORDER * STEPS
STRIP = HALO + 2
BASE = 20
ROWS = 16
CHUNKS = 13
BLOCK = 128
AGAIN = 18
GROUP = 5
TREE = (4, 2, 1)
MESH = pl.DeviceIdType.MESH
F32 = jnp.float32
BF16 = jnp.bfloat16


def halves(value):
    high = value.astype(BF16)
    return high, (value - high.astype(F32)).astype(BF16)


def build_coupling(channels, dipole, pattern, chan, square, joined, columns, lhs):
    blocks = pattern.shape[0]
    parts = square.shape[0] // BLOCK
    owned = channels // blocks
    square[...] = jnp.zeros_like(square)
    square[0:channels, 0:channels] = dipole[...]
    joined[...] = jnp.zeros_like(joined)
    joined[0:blocks, 0:blocks] = pattern[...].astype(F32)
    either = jnp.maximum(joined[...], joined[...].T).astype(BF16)
    lane = lax.broadcasted_iota(jnp.int32, (BLOCK, BLOCK), 1)
    row = lax.broadcasted_iota(jnp.int32, (BLOCK, BLOCK), 0)

    def pick(place, block):
        first = block * owned
        return jnp.where((place >= first) & (place < first + owned), 1.0, 0.0).astype(BF16)

    def spread(which, part):
        return jnp.broadcast_to(chan[which : which + 1, part * BLOCK : (part + 1) * BLOCK], (BLOCK, BLOCK))

    across = [spread(0, part) for part in range(parts)]
    picks = pick(
        lax.broadcasted_iota(jnp.int32, (BLOCK, parts * BLOCK), 1),
        lax.broadcasted_iota(jnp.int32, (BLOCK, parts * BLOCK), 0),
    )
    for i in range(parts):
        down = across[i].T
        rows = slice(i * BLOCK, (i + 1) * BLOCK)
        columns[0, rows, :] = spread(1, i).T
        columns[1, rows, :] = 0.5 * (down * (down + 1.0))
        held = jnp.dot(pick(row + i * BLOCK, lane), either, preferred_element_type=F32).astype(BF16)
        masks = jnp.dot(held, picks, preferred_element_type=F32)
        found = {}
        for j in range(parts):
            cols = slice(j * BLOCK, (j + 1) * BLOCK)
            allowed = (masks[:, cols] > 0.5) & (jnp.abs(down - across[j]) == 1.0)
            mean = 0.5 * (square[rows, cols] + square[cols, rows].T)
            coupling = jnp.where(allowed, mean, 0.0)
            high = coupling.astype(BF16).astype(F32)
            rest = coupling - high
            for copy, value in enumerate((high, high, rest)):
                place = copy * channels + j * BLOCK
                tile, off = place // BLOCK, place % BLOCK
                moved = pltpu.roll(value, off, 1) if off else value
                for tile, kept in ((tile, lane >= off), (tile + 1, lane < off)):
                    if tile in found:
                        found[tile] = found[tile] + jnp.where(kept, moved, 0.0)
                    elif tile < lhs.shape[1] // BLOCK:
                        found[tile] = jnp.where(kept, moved, 0.0)
        for tile, value in found.items():
            lhs[rows, tile * BLOCK : (tile + 1) * BLOCK] = value.astype(BF16)


def kernel(
    count, channels, states_in, dipole_in, pattern_in, angular_in, thresholds_in, prof_in, pulse, out, grad,
    to_left, to_right, from_left, from_right, strip, left_half, right_half, left_in, right_in,
    term, total, rhs, mixed, bound, surface, pot, partial, gathered,
    lhs, square, joined, columns, states, dipole, pattern, angular, thresholds, chan, prof, load,
    halo_send, halo_recv, strip_send, strip_recv, grad_send, grad_recv,
):
    me = lax.axis_index("radius")
    size = 128
    has_left, has_right = me > 0, me < count - 1
    lane = lax.broadcasted_iota(jnp.int32, (ROWS, size), 1)
    row_lane = lane[0:1, :]
    extra_rows = 16
    loads = [
        pltpu.make_async_copy(source, target, load.at[which])
        for which, (source, target) in enumerate(
            ((states_in, states), (prof_in, prof), (dipole_in, dipole), (pattern_in, pattern), (angular_in, angular), (thresholds_in, thresholds))
        )
    ]
    for copy in loads:
        copy.start()

    def over_rows(body, carry=0):
        def several(index, carry):
            for part in range(GROUP):
                carry = body(pl.multiple_of((index * GROUP + part) * ROWS, ROWS), carry)
            return carry

        return lax.fori_loop(0, channels // ROWS // GROUP, several, carry)

    barrier = pltpu.get_barrier_semaphore()

    def greet(d, _):
        other = lax.rem(me + d, count)
        pl.semaphore_signal(barrier, inc=1, device_id={"radius": other}, device_id_type=MESH)
        return 0

    lax.fori_loop(1, count, greet, 0)

    loads[0].wait()
    loads[1].wait()
    low = lane < 64
    low_quarter = (lane & 63) < 32
    padded_prof = jnp.concatenate([prof[...], jnp.zeros((extra_rows - 2, size), F32)], axis=0)
    turned_prof = pltpu.roll(padded_prof, 64, 1)

    def pack(rows, parts):
        a, b, c, d = parts
        left = jnp.where(low_quarter, jnp.where(low, a, b), pltpu.roll(jnp.where(low, c, d), 32, 1))
        right = jnp.where(low_quarter, pltpu.roll(jnp.where(low, d, c), 96, 1), jnp.where(low, b, a))
        to_left[rows, :] = left
        to_right[rows, :] = right

    def pack_rows(start, carry):
        rows = pl.ds(start, ROWS)
        a, c = states[0, rows, :], states[2, rows, :]
        b, d = pltpu.roll(states[1, rows, :], 64, 1), pltpu.roll(states[3, rows, :], 64, 1)
        pack(rows, (a, b, c, d))
        for pair, (first, other) in enumerate(((a, b), (c, d))):
            term[pair, rows, 0:size] = first
            term[pair, rows, size : 2 * size] = other
        return carry

    over_rows(pack_rows)
    pack(slice(channels, channels + extra_rows), (padded_prof, turned_prof, padded_prof, turned_prof))

    @pl.when(me == 0)
    def _():
        strip[...] = to_left[...]

    message = (channels + extra_rows) // 2
    first_half = (lane & 31) < HALO

    pl.semaphore_wait(barrier, count - 1)

    def halo_copy(source, target, which, other):
        return pltpu.make_async_remote_copy(
            src_ref=source, dst_ref=target, send_sem=halo_send.at[which],
            recv_sem=halo_recv.at[which], device_id={"radius": other}, device_id_type=MESH,
        )

    left_copy = halo_copy(left_half, right_in, 0, jnp.maximum(me - 1, 0))
    right_copy = halo_copy(right_half, left_in, 1, jnp.minimum(me + 1, count - 1))

    chunk = (channels + extra_rows) // CHUNKS
    children = []
    for step in TREE:
        child = me + step
        mine = (lax.rem(me, 2 * step) == 0) if step < TREE[0] else (lax.rem(me, step) == 0)
        children.append((child, mine & (child < count)))

    def strip_copy(part, which):
        rows = pl.ds(part * chunk, chunk)
        return pltpu.make_async_remote_copy(
            src_ref=strip.at[rows, :], dst_ref=strip.at[rows, :],
            send_sem=strip_send.at[which, part], recv_sem=strip_recv.at[part],
            device_id={"radius": jnp.minimum(children[which][0], count - 1)}, device_id_type=MESH,
        )

    def send_on(part):
        for which in range(len(TREE)):
            @pl.when(children[which][1])
            def _():
                strip_copy(part, which).start()

    @pl.when(me == 0)
    def _():
        for part in range(CHUNKS):
            send_on(part)

    def squeeze(index, _):
        near_rows = pl.ds(pl.multiple_of(index * ROWS, ROWS), ROWS)
        far_rows = pl.ds(pl.multiple_of(message + index * ROWS, ROWS), ROWS)
        left_half[near_rows, :] = jnp.where(first_half, to_left[near_rows, :], pltpu.roll(to_left[far_rows, :], HALO, 1))
        right_half[near_rows, :] = jnp.where(
            first_half, pltpu.roll(to_right[far_rows, :], size - HALO, 1), to_right[near_rows, :]
        )
        return 0

    lax.fori_loop(0, message // ROWS, squeeze, 0)

    @pl.when(has_left)
    def _():
        left_copy.start()

    @pl.when(has_right)
    def _():
        right_copy.start()

    for copy in loads[2:]:
        copy.wait()
    chan[...] = jnp.zeros_like(chan)
    chan[0:1, 0:channels] = angular[...].astype(F32)
    chan[1:2, 0:channels] = thresholds[...]
    second = (lane >= 48) & (lane < 112)
    place = jnp.where(second, ((lane + 64) & (size - 1)), lane)
    in_right, in_left = place < HALO, place >= size - HALO
    in_strip = (place >= BASE) & (place < BASE + STRIP)
    here = me * size
    extra = jnp.where(in_right, here + size + place, jnp.where(in_left, here - size + place, place - BASE))
    valid = (in_right & has_right) | (in_left & has_left) | in_strip
    extra = jnp.where(valid, extra, 0)
    keep = jnp.where(valid, 1.0, 0.0).astype(F32)
    flip = jnp.where(second, -keep, keep)
    positions = jnp.concatenate([here + row_lane, here + ((row_lane + 64) & (size - 1)), extra[0:1, :]], axis=1)
    radial = inner_radius + (positions + 1).astype(F32) * spacing
    inverse = 1.0 / (radial * radial)

    unit = 0.5 / (spacing * spacing) / 12.0
    row = lax.broadcasted_iota(jnp.int32, (size, 1), 0)
    def wide(pair, tile):
        first = 4 * size + pair * size if tile == 2 else 2 * pair * size + tile * size
        return slice(first, first + size)

    near = ((lane & 63) >= BASE) & ((lane & 63) < BASE + 4)

    def store_tile(pair, tile, start, value):
        cols = wide(pair, tile)
        high, rest = halves(value)
        if tile == 2:
            again = pltpu.roll(jnp.where(near, high.astype(F32), 0.0), AGAIN, 1)
            high = (high.astype(F32) + again).astype(BF16)
        rhs[pl.ds(start, ROWS), cols] = high
        rhs[pl.ds(channels + start, ROWS), cols] = rest
        rhs[pl.ds(2 * channels + start, ROWS), cols] = high

    def store_split(pair, start, tiles):
        for tile, value in enumerate(tiles):
            store_tile(pair, tile, start, value)

    def chain(index):
        tile, at = index >> 7, index & (size - 1)
        half = (at + 64) & (size - 1)
        other = (at >= 48) & (at < 112)
        spot = jnp.where(other, half, at)
        place = jnp.where(spot < HALO, spot + size, jnp.where(spot >= size - HALO, spot - size, 1000 + spot))
        inside = (spot < BASE + STRIP) | (spot >= size - HALO)
        inside = inside & ((spot < HALO) | (spot >= BASE))
        place = jnp.where(inside, place + jnp.where(other, 4000, 0), 10000 + 10 * at)
        return jnp.where(tile == 0, at, jnp.where(tile == 1, 4000 + half, place))

    across = chain(lax.broadcasted_iota(jnp.int32, (1, 3 * size), 1))
    def band_rows(tile):
        apart = jnp.abs(chain(row + tile * size) - across)
        return jnp.where(apart == 2, 1.0, jnp.where(apart == 1, -16.0, 0.0))

    def store_band(tile, value):
        for copy in range(2):
            first = (3 * copy + tile) * size
            surface[first : first + size, :] = value

    diagonal = 1.25 / (spacing * spacing) / unit

    def begin(start, carry):
        rows = pl.ds(start, ROWS)
        for tile in range(3):
            cols = slice(tile * size, (tile + 1) * size)
            level = columns[0, rows, :] + columns[1, rows, :] * inverse[:, cols]
            pot[rows, cols] = level / unit + diagonal
        for pair in range(2):
            for tile in range(2):
                cols = slice(tile * size, (tile + 1) * size)
                value = term[pair, rows, cols]
                store_tile(pair, tile, start, value)
                total[0, pair, rows, cols] = value
            total[1, pair, rows, :] = jnp.zeros((ROWS, 3 * size), F32)
        return carry

    pass_first = me == TREE[0]
    build_phase = jnp.where(pass_first, 1, 0)

    def phase(which, _):
        @pl.when(which == build_phase)
        def _():
            build_coupling(channels, dipole, pattern, chan, square, joined, columns, lhs)
            for tile in range(2):
                store_band(tile, band_rows(tile).astype(BF16))
            rhs[3 * channels :, :] = jnp.zeros((rhs.shape[0] - 3 * channels, 6 * size), BF16)
            over_rows(begin)

        @pl.when((which != build_phase) & (me > 0))
        def _():
            for part in range(CHUNKS):
                strip_copy(part, 0).wait_recv()
                send_on(part)

        return 0

    lax.fori_loop(0, 2, phase, 0)

    @pl.when(has_right)
    def _():
        left_copy_in = halo_copy(left_half, right_in, 0, jnp.minimum(me + 1, count - 1))
        left_copy_in.wait_recv()

    @pl.when(jnp.logical_not(has_right))
    def _():
        right_in[...] = jnp.zeros_like(right_in)

    @pl.when(has_left)
    def _():
        right_copy_in = halo_copy(right_half, left_in, 1, jnp.maximum(me - 1, 0))
        right_copy_in.wait_recv()

    @pl.when(jnp.logical_not(has_left))
    def _():
        left_in[...] = jnp.zeros_like(left_in)

    def stretch(index, _):
        near_rows = pl.ds(pl.multiple_of(index * ROWS, ROWS), ROWS)
        far_rows = pl.ds(pl.multiple_of(message + index * ROWS, ROWS), ROWS)
        right, left = right_in[near_rows, :], left_in[near_rows, :]
        from_right[near_rows, :] = right
        from_right[far_rows, :] = pltpu.roll(right, size - HALO, 1)
        from_left[near_rows, :] = left
        from_left[far_rows, :] = pltpu.roll(left, HALO, 1)
        return 0

    lax.fori_loop(0, message // ROWS, stretch, 0)

    def unpack(cut, pair):
        right, left, inner = from_right[cut, :], from_left[cut, :], strip[cut, :]
        if pair == 1:
            right, left = pltpu.roll(right, 96, 1), pltpu.roll(left, 32, 1)
        inner = pltpu.roll(inner, BASE if pair == 0 else BASE + 96, 1)
        found = jnp.where(in_right, right, jnp.where(in_left, left, inner))
        return jnp.where(valid, found, 0.0)

    def shift(value, amount):
        return pltpu.roll(value, amount % size, 1)

    prof_extra = unpack(slice(channels, channels + extra_rows), 0)
    prof_all = jnp.concatenate([padded_prof, turned_prof, prof_extra], axis=1)
    spot = row & 63
    again = (spot >= BASE + AGAIN) & (spot < BASE + AGAIN + 4)
    point = spot - BASE
    def weights(values):
        found = jnp.zeros((size, 1), F32)
        for index, value in enumerate(values):
            found = jnp.where(point == index, value / unit, found)
        return found

    value_weight = weights((4.0, -6.0, 4.0, -1.0))
    slope_weight = weights((-13.0 / 3.0, 9.5, -7.0, 11.0 / 6.0))
    owner = jnp.concatenate([jnp.zeros((1, size), jnp.int32), jnp.ones((1, size), jnp.int32), jnp.where(second, 1, 0)[0:1, :]], axis=1)
    full = value_weight * prof_all[0:1, :] + slope_weight * prof_all[1:2, :]
    full = jnp.where((row >> 6) == owner, full, 0.0)

    band = band_rows(2) + full
    high = band.astype(BF16)
    low_part = pltpu.roll(band - high.astype(F32), AGAIN, 0)
    store_band(2, jnp.where(again, low_part, high.astype(F32)).astype(BF16))

    def begin_extra(start, carry):
        rows = pl.ds(start, ROWS)
        for pair in range(2):
            value = unpack(rows, pair)
            term[pair, rows, 2 * size :] = value
            total[0, pair, rows, 2 * size :] = value
            store_tile(pair, 2, start, value)
        return carry

    over_rows(begin_extra)

    def grad_copy(other, slot):
        return pltpu.make_async_remote_copy(
            src_ref=partial, dst_ref=gathered.at[slot], send_sem=grad_send.at[other],
            recv_sem=grad_recv.at[slot], device_id={"radius": other}, device_id_type=MESH,
        )

    def one_step(step, _):
        strength = pulse[step]
        driven = (strength / unit) * radial

        def one_term(index, _):
            power = index + 1
            scale = unit * time_step / power.astype(F32)
            odd = lax.rem(power, 2)
            signed = jnp.where(odd == 1, -scale, scale)

            stacked = []
            for pair in range(2):
                tiles = [rhs[part : part + channels, wide(pair, tile)] for part in (0, channels) for tile in range(3)]
                stacked.append(jnp.concatenate(tiles, axis=1))
            bound[...] = jnp.dot(jnp.concatenate(stacked, axis=0), surface[...], preferred_element_type=F32)

            def mix(block):
                cols = slice(block * 2 * size, (block + 1) * 2 * size)
                mixed[:, cols] = jnp.dot(lhs[0:channels, :], rhs[:, cols], preferred_element_type=F32)

            mix(0)

            @pl.when(index == 0)
            def _():
                def meet(start, found):
                    rows = pl.ds(start, ROWS)
                    turned = shift(mixed[rows, size : 2 * size], 64) * term[1, rows, 0:size]
                    straight = shift(term[1, rows, size : 2 * size], 64) * mixed[rows, 0:size]
                    both = turned - straight
                    return found + both[0:8] + both[8:16]

                partial[step] = over_rows(meet, jnp.zeros((8, size), F32)) * radial[:, 0:size]

                @pl.when(step == STEPS - 1)
                def _():
                    def send(d, _):
                        grad_copy(lax.rem(me + d, count), me).start()
                        return 0

                    lax.fori_loop(1, count, send, 0)

            def advance(pair, tile):
                cols = slice(tile * size, (tile + 1) * size)
                factor = (signed, -signed, signed * flip)[tile]
                spread_driven = jnp.broadcast_to(driven[:, cols], (ROWS, size))
                for start in range(0, channels, ROWS):
                    rows = slice(start, start + ROWS)
                    value = bound[pair * channels + start : pair * channels + start + ROWS, cols]
                    value = value + pot[rows, cols] * term[pair, rows, cols]
                    value = value + spread_driven * mixed[rows, wide(pair, tile)]
                    value = factor * value
                    term[pair, rows, cols] = value
                    total[odd, pair, rows, cols] += value
                    store_tile(pair, tile, start, value)

            mix(1)
            advance(0, 0)
            advance(0, 1)
            mix(2)
            advance(1, 0)
            advance(1, 1)
            advance(0, 2)
            advance(1, 2)
            return 0

        lax.fori_loop(0, ORDER, one_term, 0)

        def close(start, carry):
            rows = pl.ds(start, ROWS)
            for pair in range(2):
                tiles = []
                for tile in range(3):
                    cols = slice(tile * size, (tile + 1) * size)
                    source = (1, 0, 2)[tile]
                    turned = shift(total[1, pair, rows, source * size : (source + 1) * size], 64)
                    tiles.append(total[0, pair, rows, cols] + turned)
                for tile in range(3):
                    cols = slice(tile * size, (tile + 1) * size)
                    term[pair, rows, cols] = tiles[tile]
                    total[0, pair, rows, cols] = tiles[tile]
                    total[1, pair, rows, cols] = jnp.zeros((ROWS, size), F32)
                store_split(pair, start, tiles)
            return carry

        over_rows(close)
        return 0

    lax.fori_loop(0, STEPS, one_step, 0)

    def finish_rows(start, carry):
        rows = pl.ds(start, ROWS)
        for pair in range(2):
            out[2 * pair, rows, :] = term[pair, rows, 0:size]
            out[2 * pair + 1, rows, :] = shift(term[pair, rows, size : 2 * size], 64)
        return carry

    over_rows(finish_rows)

    gathered[me] = partial[...]

    def collect(d, _):
        other = lax.rem(me + d, count)
        copy = grad_copy(other, other)
        copy.wait_recv()
        return 0

    lax.fori_loop(1, count, collect, 0)
    normalizer = math.sqrt(channels * count * size) * (inner_radius + count * size * spacing)
    for step in range(STEPS):
        found = jnp.zeros((8, size), F32)
        for index in range(count):
            found = found + gathered[index, step]
        grad[step] = jnp.sum(found) / normalizer

    def finish(d, _):
        grad_copy(lax.rem(me + d, count), me).wait_send()
        return 0

    lax.fori_loop(1, count, finish, 0)

    @pl.when(has_left)
    def _():
        left_copy.wait_send()

    @pl.when(has_right)
    def _():
        right_copy.wait_send()

    for which in range(len(TREE)):
        @pl.when(children[which][1])
        def _():
            for part in range(CHUNKS):
                strip_copy(part, which).wait_send()


def per_device(count, states, dipole, pattern, angular, thresholds, surface_profile, pulse_field):
    channels = states.shape[1]
    size = states.shape[2]
    padded = -(-channels // BLOCK) * BLOCK
    depth = -(-3 * channels // 256) * 256
    angular, thresholds = angular[None, :], thresholds[None, :]
    vmem = pl.BlockSpec(memory_space=pltpu.VMEM)
    smem = pl.BlockSpec(memory_space=pltpu.SMEM)
    message = pltpu.VMEM((channels + 16, size), F32)
    half = pltpu.VMEM(((channels + 16) // 2, size), F32)
    wide = (2, channels, 3 * size)
    return pl.pallas_call(
        functools.partial(kernel, count, channels),
        out_shape=(
            jax.ShapeDtypeStruct(states.shape, F32),
            jax.ShapeDtypeStruct(pulse_field.shape, F32),
        ),
        in_specs=[pl.BlockSpec(memory_space=pltpu.HBM)] * 6 + [smem],
        out_specs=(vmem, smem),
        scratch_shapes=[
            message, message, message, message, message, half, half, half, half,
            pltpu.VMEM(wide, F32),
            pltpu.VMEM((2,) + wide, F32),
            pltpu.VMEM((depth, 6 * size), BF16),
            pltpu.VMEM((channels, 6 * size), F32),
            pltpu.VMEM((2 * channels, 3 * size), F32),
            pltpu.VMEM((6 * size, 3 * size), BF16),
            pltpu.VMEM((channels, 3 * size), F32),
            pltpu.VMEM((STEPS, 8, size), F32),
            pltpu.VMEM((count, STEPS, 8, size), F32),
            pltpu.VMEM((padded, depth), BF16),
            pltpu.VMEM((padded, padded), F32),
            pltpu.VMEM((BLOCK, BLOCK), F32),
            pltpu.VMEM((2, padded, BLOCK), F32),
            pltpu.VMEM(states.shape, F32),
            pltpu.VMEM(dipole.shape, F32),
            pltpu.VMEM(pattern.shape, jnp.int32),
            pltpu.VMEM(angular.shape, jnp.int32),
            pltpu.VMEM(thresholds.shape, F32),
            pltpu.VMEM((8, padded), F32),
            pltpu.VMEM(surface_profile.shape, F32),
            pltpu.SemaphoreType.DMA((6,)),
            pltpu.SemaphoreType.DMA((2,)),
            pltpu.SemaphoreType.DMA((2,)),
            pltpu.SemaphoreType.DMA((len(TREE), CHUNKS)),
            pltpu.SemaphoreType.DMA((CHUNKS,)),
            pltpu.SemaphoreType.DMA((count,)),
            pltpu.SemaphoreType.DMA((count,)),
        ],
        compiler_params=pltpu.CompilerParams(
            collective_id=0, has_side_effects=True, vmem_limit_bytes=63 * 1024 * 1024
        ),
        cost_estimate=pl.CostEstimate(flops=8000000000, bytes_accessed=4000000, transcendentals=0),
    )(states, dipole, pattern, angular, thresholds, surface_profile, pulse_field)


def solution(mesh):
    return jax.shard_map(
        functools.partial(per_device, mesh.shape["radius"]),
        mesh=mesh,
        in_specs=(P("groups", None, "radius"), P(), P(), P(), P(), P(None, "radius"), P("groups")),
        out_specs=(P("groups", None, "radius"), P("groups")),
        check_vma=False,
    )
```
